32 devices in a mesh: req: 8 (over z, y), mp: 4 (over x, core).
Axes of the slice: x: 2, y: 2, z: 4, core: 2. Of those that a mesh axis runs over, the one named last changes fastest.
Arguments:
- hidden_in: bfloat16 [8192, 2048], P('req', 'mp'), may hold values from -6 to 6
- w_qkv: bfloat16 [3, 2048, 2048], P(None, 'req', 'mp'), may hold values from -0.125 to 0.125
- w_out: bfloat16 [2048, 2048], P('mp', 'req'), may hold values from -0.125 to 0.125
- attn_gain: bfloat16 [2048], replicated, may hold values from 0.099609375 to 1.8984375
- mlp_gain: bfloat16 [2048], replicated, may hold values from 0.099609375 to 1.8984375
- w_gate: bfloat16 [2048, 8192], P('req', 'mp'), may hold values from -0.125 to 0.125
- w_up: bfloat16 [2048, 8192], P('req', 'mp'), may hold values from -0.125 to 0.125
- w_down: bfloat16 [8192, 2048], P('mp', 'req'), may hold values from -0.0625 to 0.0625
- k_cache: bfloat16 [8, 4096, 2048], P('req', None, 'mp'), may hold values from -363 to 363
- v_cache: bfloat16 [8, 4096, 2048], P('req', None, 'mp'), may hold values from -6 to 6
- cache_len: int32 [8], P('req'), may hold values from 256 to 4096, as said below
Outputs:
- hidden_out: bfloat16 [8192, 2048], P('req', 'mp')
- new_keys: bfloat16 [8192, 2048], P('req', 'mp')
- new_values: bfloat16 [8192, 2048], P('req', 'mp')
The draws below stay inside these ranges and needn't reach their ends.
Inputs may be any that keep to these rules, and one draw needn't show every extreme that they name: Each request uses its first cache_len slots; later slots hold unused data. Some request's cache is full in every draw.
All inputs are finite; a program needn't handle non-finite values.
Results may differ from the reference program's by a relative error of at most 0.02.
Values may be sent and summed in bfloat16 or wider, within the bound.
A program may use at most 128 MiB of HBM per device.

```python
import jax
import jax.numpy as jnp
from jax import lax

D = 2048
HEADS = 32
HD = 64
FF = 8192
NEW = 1024
CACHE = 4096
REQUESTS = 8
TOKENS = 8192
N_MP = 4


def draw_cache_len(key, part):
    first, second = jax.random.split(jax.random.fold_in(key, 17))
    drawn = jax.random.randint(first, (REQUESTS,), CACHE // 16, CACHE + 1, dtype=jnp.int32)
    chosen = jax.random.randint(second, (), 0, REQUESTS, dtype=jnp.int32)
    return jnp.where(jnp.arange(REQUESTS, dtype=jnp.int32) == chosen, CACHE, drawn).astype(jnp.int32)


def draw_k_cache(key, part):
    noise_key = jax.random.fold_in(jax.random.fold_in(key, 29), 0)
    noise = jnp.clip(jax.random.normal(noise_key, (REQUESTS, CACHE, D), jnp.float32), -6.0, 6.0)
    return noise.astype(jnp.bfloat16)


def steps_of(stream_key, extent, cuts, smallest, largest):
    level, own = 1.0, jax.random.fold_in(stream_key, 6)
    for position, parts in cuts:
        steps = jnp.exp(jax.random.uniform(jax.random.fold_in(own, position), (parts,), jnp.float32, smallest / len(cuts), largest / len(cuts)))
        level = level * jnp.repeat(steps, extent[position] // parts).reshape([-1 if axis == position else 1 for axis in range(len(extent))])
    return level


def scatter_about(own_key, shape, scale, limit, pieces=(), kind=jnp.bfloat16):
    array = scale * jax.random.normal(own_key, shape, jnp.float32)
    if pieces:
        array = array * steps_of(own_key, shape, pieces, -0.22, 0.18)
    return jnp.clip(array, -limit, limit).astype(kind)


def setup_inputs(seed: int = 0) -> dict:
    keys = jax.random.split(jax.random.key(seed), 12)
    hidden_in = scatter_about(keys[0], (TOKENS, D), 1.0, 6.0, ((0, 8), (1, 4)))
    w_qkv = scatter_about(keys[1], (3, D, D), D ** -0.5, 0.125, ((1, 8), (2, 4)))
    w_out = scatter_about(keys[2], (D, D), D ** -0.5, 0.125, ((0, 4), (1, 8)))
    attn_gain = jnp.clip(1.0 + 0.18 * jax.random.normal(keys[3], (D,), jnp.float32), 0.099609375, 1.8984375).astype(jnp.bfloat16)
    mlp_gain = jnp.clip(1.0 + 0.18 * jax.random.normal(keys[4], (D,), jnp.float32), 0.099609375, 1.8984375).astype(jnp.bfloat16)
    w_gate = scatter_about(keys[5], (D, FF), D ** -0.5, 0.125, ((0, 8), (1, 4)))
    w_up = scatter_about(keys[6], (D, FF), D ** -0.5, 0.125, ((0, 8), (1, 4)))
    w_down = scatter_about(keys[7], (FF, D), FF ** -0.5, 0.0625, ((0, 4), (1, 8)))
    k_cache = draw_k_cache(jax.random.fold_in(keys[11], 71), 0)
    v_cache = scatter_about(keys[9], (REQUESTS, CACHE, D), 1.0, 6.0, ((0, 8), (2, 4)))
    cache_len = draw_cache_len(jax.random.fold_in(keys[11], 71), 0)
    return {"hidden_in": hidden_in, "w_qkv": w_qkv, "w_out": w_out, "attn_gain": attn_gain, "mlp_gain": mlp_gain, "w_gate": w_gate, "w_up": w_up, "w_down": w_down, "k_cache": k_cache, "v_cache": v_cache, "cache_len": cache_len}


THETA = 130000.0
EPSILON = 1e-05

def rms_scale(rows, gain):
    values = rows.astype(jnp.float32)
    meansq = lax.optimization_barrier(jnp.mean(values * values, axis=-1, keepdims=True))
    return (values * lax.rsqrt(meansq + EPSILON) * gain.astype(jnp.float32)).astype(jnp.bfloat16)

def rotate(tensor, positions):
    half = tensor.shape[-1] // 2
    freq = THETA ** (-(jnp.arange(half, dtype=jnp.float32) * 2.0 / tensor.shape[-1]))
    angle = positions[:, None, None] * freq[None, None, :]
    cosine = jnp.cos(angle)
    sine = jnp.sin(angle)
    first = tensor[..., :half]
    second = tensor[..., half:]
    return jnp.concatenate([first * cosine - second * sine, second * cosine + first * sine], axis=-1)

def grouped_sum(left, right, groups):
    width = left.shape[1] // groups
    total = jnp.zeros((left.shape[0], right.shape[1]), jnp.float32)
    for group in range(groups):
        part = jnp.dot(left[:, group * width:(group + 1) * width], right[group * width:(group + 1) * width], preferred_element_type=jnp.float32).astype(jnp.bfloat16)
        part = lax.optimization_barrier(part)
        total = total + part.astype(jnp.float32)
    return total

def reference(hidden_in, w_qkv, w_out, attn_gain, mlp_gain, w_gate, w_up, w_down, k_cache, v_cache, cache_len):
    scale = HD ** (-0.5)
    normed = rms_scale(hidden_in, attn_gain)
    proj_query = jnp.dot(normed, w_qkv[0], preferred_element_type=jnp.float32)
    proj_key = jnp.dot(normed, w_qkv[1], preferred_element_type=jnp.float32)
    proj_value = jnp.dot(normed, w_qkv[2], preferred_element_type=jnp.float32)
    offsets = jnp.repeat(cache_len.astype(jnp.int32), NEW) + jnp.tile(jnp.arange(NEW, dtype=jnp.int32), REQUESTS)
    positions = offsets.astype(jnp.float32)
    queries = rotate(proj_query.reshape(TOKENS, HEADS, HD), positions).astype(jnp.bfloat16)
    new_keys = rotate(proj_key.reshape(TOKENS, HEADS, HD), positions).astype(jnp.bfloat16)
    new_values = proj_value.astype(jnp.bfloat16).reshape(TOKENS, HEADS, HD)

    def one_request(inputs):
        req_q, req_k, req_v, cache_k, cache_v, length = inputs
        slot_ok = jnp.arange(CACHE, dtype=jnp.int32) < length
        rows = jnp.arange(NEW, dtype=jnp.int32)
        causal = rows[:, None] >= rows[None, :]
        mask = jnp.concatenate([jnp.broadcast_to(slot_ok[None, :], (NEW, CACHE)), causal], axis=1)

        def one_head(head_in):
            head_q, head_k, head_v, head_ck, head_cv = head_in
            score_c = jnp.dot(head_q, head_ck.T, preferred_element_type=jnp.float32) * scale
            score_n = jnp.dot(head_q, head_k.T, preferred_element_type=jnp.float32) * scale
            scores = jnp.where(mask, jnp.concatenate([score_c, score_n], axis=1), -1e+30)
            top = lax.optimization_barrier(jnp.max(scores, axis=1, keepdims=True))
            probs = jnp.where(mask, jnp.exp(scores - top), 0.0)
            total = lax.optimization_barrier(jnp.sum(probs, axis=1, keepdims=True))
            values = jnp.concatenate([head_cv, head_v], axis=0)
            weighted = jnp.dot(probs.astype(jnp.bfloat16), values, preferred_element_type=jnp.float32)
            return weighted / total
        per_head = lax.map(one_head, (req_q.transpose(1, 0, 2), req_k.transpose(1, 0, 2), req_v.transpose(1, 0, 2), cache_k.transpose(1, 0, 2), cache_v.transpose(1, 0, 2)))
        return per_head.transpose(1, 0, 2).reshape(NEW, D).astype(jnp.bfloat16)
    attn = lax.map(one_request, (queries.reshape(REQUESTS, NEW, HEADS, HD), new_keys.reshape(REQUESTS, NEW, HEADS, HD), new_values.reshape(REQUESTS, NEW, HEADS, HD), k_cache.reshape(REQUESTS, CACHE, HEADS, HD), v_cache.reshape(REQUESTS, CACHE, HEADS, HD), cache_len.astype(jnp.int32)))
    attn = attn.reshape(TOKENS, D)
    mid = (hidden_in.astype(jnp.float32) + grouped_sum(attn, w_out, N_MP)).astype(jnp.bfloat16)
    normed2 = rms_scale(mid, mlp_gain)
    gate = jnp.dot(normed2, w_gate, preferred_element_type=jnp.float32)
    upper = jnp.dot(normed2, w_up, preferred_element_type=jnp.float32)
    units = (jax.nn.silu(gate) * upper).astype(jnp.bfloat16)
    hidden_out = (mid.astype(jnp.float32) + grouped_sum(units, w_down, N_MP)).astype(jnp.bfloat16)
    return (hidden_out, new_keys.reshape(TOKENS, D), new_values.reshape(TOKENS, D))
```

```python
import functools

import jax
import jax.numpy as jnp
from jax import lax
from jax.experimental import pallas as pl
from jax.experimental.pallas import tpu as pltpu
from jax.sharding import PartitionSpec as P

HD = 64
MESH = pl.DeviceIdType.MESH
LOG2E = 1.4426950408889634
PAIR = 2 * HD

THETA = 130000.0
EPSILON = 1e-05
NEG_FILL = -1e30


def rms_scale(rows, gain):
    values = rows.astype(jnp.float32)
    meansq = jnp.mean(values * values, axis=-1, keepdims=True)
    return (values * lax.rsqrt(meansq + EPSILON) * gain.astype(jnp.float32)).astype(jnp.bfloat16)


def rotate(tensor, positions):
    half = tensor.shape[-1] // 2
    freq = THETA ** (-(jnp.arange(half, dtype=jnp.float32) * 2.0 / tensor.shape[-1]))
    angle = positions[:, None, None] * freq[None, None, :]
    cosine = jnp.cos(angle)
    sine = jnp.sin(angle)
    first = tensor[..., :half]
    second = tensor[..., half:]
    return jnp.concatenate(
        [first * cosine - second * sine, second * cosine + first * sine], axis=-1
    )


def columns_of(ref, index, width):
    return ref.at[:, pl.ds(pl.multiple_of(index * width, width), width)]


class ReqGather:
    def __init__(self, n, pieces, sems):
        self.half = n // 2
        self.pieces = pieces
        self.send_far, self.recv_far, self.send_near, self.recv_near, self.own_sem = sems
        me = lax.axis_index("req")
        self.group, self.parity = me // 2, lax.rem(me, 2)
        self.me, self.partner = me, me + 1 - 2 * self.parity

    def member(self, shift):
        return lax.rem(self.group + shift + self.half, self.half) * 2 + self.parity

    def greet(self, barrier):
        for shift in range(1, self.half):
            pl.semaphore_signal(barrier, inc=1, device_id={"req": self.member(shift)}, device_id_type=MESH)
        pl.semaphore_signal(barrier, inc=1, device_id={"req": self.partner}, device_id_type=MESH)
        return self.half

    def far(self, c, shift):
        src, slot = self.pieces[c]
        return pltpu.make_async_remote_copy(
            src_ref=src, dst_ref=slot(self.me), send_sem=self.send_far.at[c, shift],
            recv_sem=self.recv_far.at[c, shift], device_id={"req": self.member(shift)}, device_id_type=MESH)

    def near(self, c, shift):
        src, slot = self.pieces[c]
        owner = self.member(-shift)
        return pltpu.make_async_remote_copy(
            src_ref=src if shift == 0 else slot(owner), dst_ref=slot(owner), send_sem=self.send_near.at[c, shift],
            recv_sem=self.recv_near.at[c, shift], device_id={"req": self.partner}, device_id_type=MESH)

    def own(self, c):
        src, slot = self.pieces[c]
        return pltpu.make_async_copy(src, slot(self.me), self.own_sem.at[c])

    def start(self, c):
        for shift in range(1, self.half):
            self.far(c, shift).start()
        self.near(c, 0).start()
        self.own(c).start()

    def forward(self, c):
        for shift in range(1, self.half):
            self.far(c, shift).wait_recv()
            self.near(c, shift).start()

    def finish(self, c):
        for shift in range(1, self.half):
            self.far(c, shift).wait_send()
        for shift in range(self.half):
            self.near(c, shift).wait()
        self.own(c).wait()


def gather_sems(pieces, n):
    dma = pltpu.SemaphoreType.DMA
    return [dma((pieces, n // 2)) for _ in range(4)] + [dma((pieces,))]


def first_kernel(n, n_mp, hid, wqkv, hid_full, wqkv_full, *sems):
    mp_send, mp_recv, mp_own = sems[5:]
    depth, width = wqkv.shape[1], hid.shape[1]
    pieces = [
        (wqkv.at[i], lambda r, i=i: wqkv_full.at[i, pl.ds(pl.multiple_of(r * depth, depth), depth)])
        for i in range(3)
    ]
    gather = ReqGather(n, pieces, sems[:5])
    me = lax.axis_index("mp")
    barrier = pltpu.get_barrier_semaphore()
    expected = gather.greet(barrier)
    for shift in range(1, n_mp):
        pl.semaphore_signal(barrier, inc=1, device_id={"mp": lax.rem(me + shift, n_mp)}, device_id_type=MESH)
    pl.semaphore_wait(barrier, expected + n_mp - 1)
    mine = columns_of(hid_full, me, width)
    copies = [
        pltpu.make_async_remote_copy(
            src_ref=hid, dst_ref=mine, send_sem=mp_send.at[shift], recv_sem=mp_recv.at[shift],
            device_id={"mp": lax.rem(me + shift, n_mp)}, device_id_type=MESH)
        for shift in range(1, n_mp)
    ]
    own = pltpu.make_async_copy(hid, mine, mp_own)
    for c in range(3):
        gather.start(c)
    for copy in copies:
        copy.start()
    own.start()
    for c in range(3):
        gather.forward(c)
    for c in range(3):
        gather.finish(c)
    for copy in copies:
        copy.wait()
    own.wait()


def gather_first(n, n_mp, hidden_in, w_qkv):
    rows, width = hidden_in.shape
    dma = pltpu.SemaphoreType.DMA
    hbm = pl.BlockSpec(memory_space=pl.ANY)
    return pl.pallas_call(
        functools.partial(first_kernel, n, n_mp),
        out_shape=(
            jax.ShapeDtypeStruct((rows, width * n_mp), hidden_in.dtype),
            jax.ShapeDtypeStruct((3, w_qkv.shape[1] * n, w_qkv.shape[2]), w_qkv.dtype),
        ),
        in_specs=[hbm, hbm],
        out_specs=(hbm, hbm),
        scratch_shapes=gather_sems(3, n) + [dma((n_mp,)), dma((n_mp,)), dma],
        compiler_params=pltpu.CompilerParams(collective_id=0, has_side_effects=True),
    )(hidden_in, w_qkv)


def attend(length, q_begin, q_ref, kn_ref, vn_ref, kc_ref, vc_ref, out_ref):
    rows = q_ref.shape[0]
    fresh = kn_ref.shape[0]
    slots = kc_ref.shape[1]
    block = min(slots, 512)
    lane = lax.broadcasted_iota(jnp.int32, (1, PAIR), 1)
    masks = (lane < HD, lane >= HD)
    query = q_ref[...]
    queries = [jnp.where(mask, query, 0) for mask in masks]
    row_index = q_begin + lax.broadcasted_iota(jnp.int32, (rows, 1), 0)

    def absorb(state, keys, values, hide):
        out = []
        for mask, mine, (top, accum) in zip(masks, queries, state):
            scores = lax.dot_general(
                mine, keys, (((1,), (1,)), ((), ())), preferred_element_type=jnp.float32)
            scores = hide(scores * (LOG2E * HD**-0.5))
            new_top = jnp.maximum(top, jnp.max(scores, axis=1, keepdims=True))
            probs = jnp.exp2(scores - new_top).astype(jnp.bfloat16)
            extended = jnp.where(mask, values, 1)
            accum = accum * jnp.exp2(top - new_top) + jnp.dot(
                probs, extended, preferred_element_type=jnp.float32)
            out.append((new_top, accum))
        return tuple(out)

    state = tuple(
        (jnp.full((rows, 1), NEG_FILL, jnp.float32), jnp.zeros((rows, PAIR), jnp.float32)) for _ in masks)

    def fresh_step(index, state):
        begin = pl.multiple_of(index * block, block)
        column = begin + lax.broadcasted_iota(jnp.int32, (1, block), 1)
        return absorb(
            state, kn_ref[pl.ds(begin, block)], vn_ref[pl.ds(begin, block)],
            lambda scores: jnp.where(row_index >= column, scores, NEG_FILL))

    def cache_step(index, state):
        begin = pl.multiple_of(index * block, block)
        column = begin + lax.broadcasted_iota(jnp.int32, (1, block), 1)
        bias = jnp.where(column < length, 0.0, NEG_FILL)
        return absorb(
            state, kc_ref[0, pl.ds(begin, block)], vc_ref[0, pl.ds(begin, block)],
            lambda scores: scores + bias)

    state = lax.fori_loop(0, fresh // block, fresh_step, state)
    state = lax.fori_loop(0, slots // block, cache_step, state)
    parts = [accum / pltpu.roll(accum, HD, 1) for _, accum in state]
    out_ref[...] = jnp.where(masks[0], parts[0], parts[1]).astype(out_ref.dtype)


def attention_kernel(
    n, n_pairs, n_blocks, length_ref, q_ref, kn_ref, vn_ref, kc_ref, vc_ref, w_out, w_gate, w_up, w_down,
    out_ref, w_out_full, w_gate_full, w_up_full, w_down_full, *sems
):
    step = pl.program_id(0) * n_blocks + pl.program_id(1)
    steps = n_pairs * n_blocks
    pieces = [(w_out, lambda r: columns_of(w_out_full, r, w_out.shape[1]))]
    for src, full in ((w_gate, w_gate_full), (w_up, w_up_full)):
        depth = src.shape[0]
        for part in range(2):
            rows = depth // 2
            pieces.append((
                src.at[pl.ds(part * rows, rows)],
                lambda r, full=full, part=part, depth=depth, rows=rows: full.at[
                    pl.ds(pl.multiple_of(r * depth + part * rows, rows), rows)]))
    for part in range(2):
        rows, width = w_down.shape[0] // 2, w_down.shape[1]
        pieces.append((
            w_down.at[pl.ds(part * rows, rows)],
            lambda r, part=part, rows=rows, width=width: w_down_full.at[
                pl.ds(part * rows, rows), pl.ds(pl.multiple_of(r * width, width), width)]))
    gather = ReqGather(n, pieces, sems)
    count = len(pieces)

    @pl.when(step == 0)
    def _():
        barrier = pltpu.get_barrier_semaphore()
        pl.semaphore_wait(barrier, gather.greet(barrier))
        for c in range(3):
            gather.start(c)

    attend(
        length_ref[0], pl.program_id(1) * q_ref.shape[0], q_ref, kn_ref, vn_ref, kc_ref, vc_ref, out_ref)

    for c in range(count):
        @pl.when(step == min(c, steps - 1))
        def _(c=c):
            gather.forward(c)
            if c + 3 < count:
                gather.start(c + 3)

    @pl.when(step == steps - 1)
    def _():
        for c in range(count):
            gather.finish(c)


def attend_and_gather(n, length, queries, keys, values, k_cache, v_cache, w_out, w_gate, w_up, w_down):
    rows, width = queries.shape
    slots = k_cache.shape[1]
    n_pairs, n_blocks = width // PAIR, 2
    hbm = pl.BlockSpec(memory_space=pl.ANY)
    row_block = pl.BlockSpec((rows // n_blocks, PAIR), lambda h, i: (i, h))
    whole = pl.BlockSpec((rows, PAIR), lambda h, i: (0, h))
    cached = pl.BlockSpec((1, slots, PAIR), lambda h, i: (0, 0, h))
    like = jax.ShapeDtypeStruct
    return pl.pallas_call(
        functools.partial(attention_kernel, n, n_pairs, n_blocks),
        grid=(n_pairs, n_blocks),
        out_shape=(
            like((rows, width), queries.dtype),
            like((w_out.shape[0], w_out.shape[1] * n), w_out.dtype),
            like((w_gate.shape[0] * n, w_gate.shape[1]), w_gate.dtype),
            like((w_up.shape[0] * n, w_up.shape[1]), w_up.dtype),
            like((w_down.shape[0], w_down.shape[1] * n), w_down.dtype),
        ),
        in_specs=[pl.BlockSpec(memory_space=pltpu.SMEM), row_block, whole, whole, cached, cached] + [hbm] * 4,
        out_specs=(row_block,) + (hbm,) * 4,
        scratch_shapes=gather_sems(7, n),
        compiler_params=pltpu.CompilerParams(
            collective_id=1, has_side_effects=True, vmem_limit_bytes=48 * 1024 * 1024,
            dimension_semantics=("arbitrary", "arbitrary")),
    )(length, queries, keys, values, k_cache, v_cache, w_out, w_gate, w_up, w_down)


def on_device(
    n, n_mp, hidden_in, w_qkv, w_out, attn_gain, mlp_gain, w_gate, w_up, w_down, k_cache, v_cache, cache_len
):
    new_count = hidden_in.shape[0]
    width = w_qkv.shape[2]
    heads_local = width // HD
    full_rows, w_qkv_full = gather_first(n, n_mp, hidden_in, w_qkv)
    normed = rms_scale(full_rows, attn_gain)
    columns = normed
    projected = jnp.einsum(
        "nd,kdw->knw",
        columns,
        w_qkv_full,
        preferred_element_type=jnp.float32,
    )
    length = cache_len[0]
    positions = (length + jnp.arange(new_count, dtype=jnp.int32)).astype(jnp.float32)
    queries = rotate(projected[0].reshape(new_count, heads_local, HD), positions).astype(
        jnp.bfloat16
    )
    fresh_keys = rotate(projected[1].reshape(new_count, heads_local, HD), positions).astype(
        jnp.bfloat16
    )
    fresh_values = projected[2].astype(jnp.bfloat16).reshape(new_count, heads_local, HD)
    attn, w_out_full, w_gate_full, w_up_full, w_down_full = attend_and_gather(
        n, cache_len, queries.reshape(new_count, width), fresh_keys.reshape(new_count, width),
        fresh_values.reshape(new_count, width), k_cache, v_cache, w_out, w_gate, w_up, w_down)
    partial_value = jnp.dot(
        attn, w_out_full, preferred_element_type=jnp.float32
    )
    summed = lax.psum_scatter(
        partial_value.astype(jnp.bfloat16), "mp", scatter_dimension=1, tiled=True
    ).astype(jnp.float32)
    mid_local = (hidden_in.astype(jnp.float32) + summed).astype(jnp.bfloat16)
    mid_full = lax.all_gather(mid_local, "mp", axis=1, tiled=True)
    normed2 = rms_scale(mid_full, mlp_gain)
    columns = normed2
    gate = jnp.dot(
        columns,
        w_gate_full,
        preferred_element_type=jnp.float32,
    )
    upper = jnp.dot(
        columns, w_up_full, preferred_element_type=jnp.float32
    )
    units = (jax.nn.silu(gate) * upper).astype(jnp.bfloat16)
    terms = jnp.dot(
        units, w_down_full, preferred_element_type=jnp.float32
    )
    reduced = lax.psum_scatter(
        terms.astype(jnp.bfloat16), "mp", scatter_dimension=1, tiled=True
    ).astype(jnp.float32)
    hidden_out = (mid_local.astype(jnp.float32) + reduced).astype(jnp.bfloat16)
    return (
        hidden_out,
        fresh_keys.reshape(new_count, width),
        fresh_values.reshape(new_count, width),
    )


def solution(mesh):
    return jax.shard_map(
        functools.partial(on_device, mesh.shape["req"], mesh.shape["mp"]),
        mesh=mesh,
        in_specs=(
            P("req", "mp"),
            P(None, "req", "mp"),
            P("mp", "req"),
            P(),
            P(),
            P("req", "mp"),
            P("req", "mp"),
            P("mp", "req"),
            P("req", None, "mp"),
            P("req", None, "mp"),
            P("req"),
        ),
        out_specs=(P("req", "mp"), P("req", "mp"), P("req", "mp")),
        check_vma=False,
    )
```

```python
import functools

import jax
import jax.numpy as jnp
from jax import lax
from jax.experimental import pallas as pl
from jax.experimental.pallas import tpu as pltpu
from jax.sharding import PartitionSpec as P

HD = 64
MESH = pl.DeviceIdType.MESH
LOG2E = 1.4426950408889634
PAIR = 2 * HD

THETA = 130000.0
EPSILON = 1e-05
NEG_FILL = -1e30


def rms_scale(rows, gain):
    values = rows.astype(jnp.float32)
    meansq = jnp.mean(values * values, axis=-1, keepdims=True)
    return (values * lax.rsqrt(meansq + EPSILON) * gain.astype(jnp.float32)).astype(jnp.bfloat16)


def rotate(tensor, positions):
    half = tensor.shape[-1] // 2
    freq = THETA ** (-(jnp.arange(half, dtype=jnp.float32) * 2.0 / tensor.shape[-1]))
    angle = positions[:, None, None] * freq[None, None, :]
    cosine = jnp.cos(angle)
    sine = jnp.sin(angle)
    first = tensor[..., :half]
    second = tensor[..., half:]
    return jnp.concatenate(
        [first * cosine - second * sine, second * cosine + first * sine], axis=-1
    )


def columns_of(ref, index, width):
    return ref.at[:, pl.ds(pl.multiple_of(index * width, width), width)]


class Gather:
    def __init__(self, axis, n, pieces, sems):
        self.axis = axis
        self.half = n // 2
        self.pieces = pieces
        self.send_far, self.recv_far, self.send_near, self.recv_near, self.own_sem = sems
        me = lax.axis_index(axis)
        self.group, self.parity = me // 2, lax.rem(me, 2)
        self.me, self.partner = me, me + 1 - 2 * self.parity

    def member(self, shift):
        return lax.rem(self.group + shift + self.half, self.half) * 2 + self.parity

    def greet(self, barrier):
        for shift in range(1, self.half):
            pl.semaphore_signal(barrier, inc=1, device_id={self.axis: self.member(shift)}, device_id_type=MESH)
        pl.semaphore_signal(barrier, inc=1, device_id={self.axis: self.partner}, device_id_type=MESH)
        return self.half

    def far(self, c, shift):
        src, slot = self.pieces[c]
        return pltpu.make_async_remote_copy(
            src_ref=src, dst_ref=slot(self.me), send_sem=self.send_far.at[c, shift],
            recv_sem=self.recv_far.at[c, shift], device_id={self.axis: self.member(shift)}, device_id_type=MESH)

    def near(self, c, shift):
        src, slot = self.pieces[c]
        owner = self.member(-shift)
        return pltpu.make_async_remote_copy(
            src_ref=src if shift == 0 else slot(owner), dst_ref=slot(owner), send_sem=self.send_near.at[c, shift],
            recv_sem=self.recv_near.at[c, shift], device_id={self.axis: self.partner}, device_id_type=MESH)

    def own(self, c):
        src, slot = self.pieces[c]
        return pltpu.make_async_copy(src, slot(self.me), self.own_sem.at[c])

    def start(self, c):
        for shift in range(1, self.half):
            self.far(c, shift).start()
        self.near(c, 0).start()
        if self.own_sem is not None:
            self.own(c).start()

    def forward(self, c):
        for shift in range(1, self.half):
            self.far(c, shift).wait_recv()
            self.near(c, shift).start()

    def finish(self, c):
        for shift in range(1, self.half):
            self.far(c, shift).wait_send()
        for shift in range(self.half):
            self.near(c, shift).wait()
        if self.own_sem is not None:
            self.own(c).wait()


def gather_sems(pieces, n):
    dma = pltpu.SemaphoreType.DMA
    return [dma((pieces, n // 2)) for _ in range(4)] + [dma((pieces,))]


def first_kernel(n, n_mp, hid, wqkv, hid_full, wqkv_full, *sems):
    mp_send, mp_recv, mp_own = sems[5:]
    depth, width = wqkv.shape[1], hid.shape[1]
    pieces = [
        (wqkv.at[i], lambda r, i=i: wqkv_full.at[i, pl.ds(pl.multiple_of(r * depth, depth), depth)])
        for i in range(3)
    ]
    gather = Gather("req", n, pieces, sems[:5])
    me = lax.axis_index("mp")
    barrier = pltpu.get_barrier_semaphore()
    expected = gather.greet(barrier)
    for shift in range(1, n_mp):
        pl.semaphore_signal(barrier, inc=1, device_id={"mp": lax.rem(me + shift, n_mp)}, device_id_type=MESH)
    pl.semaphore_wait(barrier, expected + n_mp - 1)
    mine = columns_of(hid_full, me, width)
    copies = [
        pltpu.make_async_remote_copy(
            src_ref=hid, dst_ref=mine, send_sem=mp_send.at[shift], recv_sem=mp_recv.at[shift],
            device_id={"mp": lax.rem(me + shift, n_mp)}, device_id_type=MESH)
        for shift in range(1, n_mp)
    ]
    own = pltpu.make_async_copy(hid, mine, mp_own)
    for c in range(3):
        gather.start(c)
    for copy in copies:
        copy.start()
    own.start()
    for c in range(3):
        gather.forward(c)
    for c in range(3):
        gather.finish(c)
    for copy in copies:
        copy.wait()
    own.wait()


def gather_first(n, n_mp, hidden_in, w_qkv):
    rows, width = hidden_in.shape
    dma = pltpu.SemaphoreType.DMA
    hbm = pl.BlockSpec(memory_space=pl.ANY)
    return pl.pallas_call(
        functools.partial(first_kernel, n, n_mp),
        out_shape=(
            jax.ShapeDtypeStruct((rows, width * n_mp), hidden_in.dtype),
            jax.ShapeDtypeStruct((3, w_qkv.shape[1] * n, w_qkv.shape[2]), w_qkv.dtype),
        ),
        in_specs=[hbm, hbm],
        out_specs=(hbm, hbm),
        scratch_shapes=gather_sems(3, n) + [dma((n_mp,)), dma((n_mp,)), dma],
        compiler_params=pltpu.CompilerParams(collective_id=0, has_side_effects=True),
    )(hidden_in, w_qkv)


def attend(length, q_begin, q_ref, kn_ref, vn_ref, kc_ref, vc_ref, out_ref):
    rows = q_ref.shape[0]
    fresh = kn_ref.shape[0]
    slots = kc_ref.shape[1]
    block = min(slots, 512)
    lane = lax.broadcasted_iota(jnp.int32, (1, PAIR), 1)
    masks = (lane < HD, lane >= HD)
    query = q_ref[...]
    queries = [jnp.where(mask, query, 0) for mask in masks]
    row_index = q_begin + lax.broadcasted_iota(jnp.int32, (rows, 1), 0)

    def absorb(state, keys, values, hide):
        out = []
        for mask, mine, (top, accum) in zip(masks, queries, state):
            scores = lax.dot_general(
                mine, keys, (((1,), (1,)), ((), ())), preferred_element_type=jnp.float32)
            scores = hide(scores * (LOG2E * HD**-0.5))
            new_top = jnp.maximum(top, jnp.max(scores, axis=1, keepdims=True))
            probs = jnp.exp2(scores - new_top).astype(jnp.bfloat16)
            extended = jnp.where(mask, values, 1)
            accum = accum * jnp.exp2(top - new_top) + jnp.dot(
                probs, extended, preferred_element_type=jnp.float32)
            out.append((new_top, accum))
        return tuple(out)

    state = tuple(
        (jnp.full((rows, 1), NEG_FILL, jnp.float32), jnp.zeros((rows, PAIR), jnp.float32)) for _ in masks)

    def fresh_step(index, state):
        begin = pl.multiple_of(index * block, block)
        column = begin + lax.broadcasted_iota(jnp.int32, (1, block), 1)
        return absorb(
            state, kn_ref[pl.ds(begin, block)], vn_ref[pl.ds(begin, block)],
            lambda scores: jnp.where(row_index >= column, scores, NEG_FILL))

    def cache_step(index, state):
        begin = pl.multiple_of(index * block, block)
        column = begin + lax.broadcasted_iota(jnp.int32, (1, block), 1)
        bias = jnp.where(column < length, 0.0, NEG_FILL)
        return absorb(
            state, kc_ref[0, pl.ds(begin, block)], vc_ref[0, pl.ds(begin, block)],
            lambda scores: scores + bias)

    state = lax.fori_loop(0, fresh // block, fresh_step, state)
    state = lax.fori_loop(0, slots // block, cache_step, state)
    parts = [accum / pltpu.roll(accum, HD, 1) for _, accum in state]
    out_ref[...] = jnp.where(masks[0], parts[0], parts[1]).astype(out_ref.dtype)


def attention_kernel(
    n, n_pairs, n_blocks, length_ref, q_ref, kn_ref, vn_ref, kc_ref, vc_ref, w_out, w_gate, w_up,
    out_ref, w_out_full, w_gate_full, w_up_full, *sems
):
    step = pl.program_id(0) * n_blocks + pl.program_id(1)
    steps = n_pairs * n_blocks
    pieces = [(w_out, lambda r: columns_of(w_out_full, r, w_out.shape[1]))]
    for src, full in ((w_gate, w_gate_full), (w_up, w_up_full)):
        depth = src.shape[0]
        for part in range(2):
            rows = depth // 2
            pieces.append((
                src.at[pl.ds(part * rows, rows)],
                lambda r, full=full, part=part, depth=depth, rows=rows: full.at[
                    pl.ds(pl.multiple_of(r * depth + part * rows, rows), rows)]))
    gather = Gather("req", n, pieces, sems)
    count = len(pieces)

    @pl.when(step == 0)
    def _():
        barrier = pltpu.get_barrier_semaphore()
        pl.semaphore_wait(barrier, gather.greet(barrier))
        for c in range(3):
            gather.start(c)

    attend(
        length_ref[0], pl.program_id(1) * q_ref.shape[0], q_ref, kn_ref, vn_ref, kc_ref, vc_ref, out_ref)

    for c in range(count):
        @pl.when(step == min(c, steps - 1))
        def _(c=c):
            gather.forward(c)
            if c + 3 < count:
                gather.start(c + 3)

    @pl.when(step == steps - 1)
    def _():
        for c in range(count):
            gather.finish(c)


def attend_and_gather(n, length, queries, keys, values, k_cache, v_cache, w_out, w_gate, w_up):
    rows, width = queries.shape
    slots = k_cache.shape[1]
    n_pairs, n_blocks = width // PAIR, 2
    hbm = pl.BlockSpec(memory_space=pl.ANY)
    row_block = pl.BlockSpec((rows // n_blocks, PAIR), lambda h, i: (i, h))
    whole = pl.BlockSpec((rows, PAIR), lambda h, i: (0, h))
    cached = pl.BlockSpec((1, slots, PAIR), lambda h, i: (0, 0, h))
    like = jax.ShapeDtypeStruct
    return pl.pallas_call(
        functools.partial(attention_kernel, n, n_pairs, n_blocks),
        grid=(n_pairs, n_blocks),
        out_shape=(
            like((rows, width), queries.dtype),
            like((w_out.shape[0], w_out.shape[1] * n), w_out.dtype),
            like((w_gate.shape[0] * n, w_gate.shape[1]), w_gate.dtype),
            like((w_up.shape[0] * n, w_up.shape[1]), w_up.dtype),
        ),
        in_specs=[pl.BlockSpec(memory_space=pltpu.SMEM), row_block, whole, whole, cached, cached] + [hbm] * 3,
        out_specs=(row_block,) + (hbm,) * 3,
        scratch_shapes=gather_sems(5, n),
        compiler_params=pltpu.CompilerParams(
            collective_id=1, has_side_effects=True, vmem_limit_bytes=48 * 1024 * 1024,
            dimension_semantics=("arbitrary", "arbitrary")),
    )(length, queries, keys, values, k_cache, v_cache, w_out, w_gate, w_up)


CHUNKS = 4
DOWN_PIECES = 4


class Reduce:
    def __init__(self, n, part, near_in, far_out, far_in, sems):
        self.half, self.part, self.near_in, self.far_out, self.far_in = n // 2, part, near_in, far_out, far_in
        self.near_send, self.near_recv, self.far_send, self.far_recv = sems
        self.me = lax.axis_index("mp")
        self.group, self.parity = self.me // 2, lax.rem(self.me, 2)
        self.partner = self.me + 1 - 2 * self.parity
        self.width = part.shape[1] // n
        self.rows = part.shape[0] // CHUNKS

    def rows_of(self, c):
        return pl.ds(c * self.rows, self.rows)

    def block(self, c, index):
        return self.part.at[
            self.rows_of(c), pl.ds(pl.multiple_of(index * self.width, self.width), self.width)]

    def near(self, c, g):
        return pltpu.make_async_remote_copy(
            src_ref=self.block(c, g * 2 + 1 - self.parity), dst_ref=self.near_in.at[g, self.rows_of(c)],
            send_sem=self.near_send.at[c, g], recv_sem=self.near_recv.at[c, g],
            device_id={"mp": self.partner}, device_id_type=MESH)

    def far(self, c, shift):
        target = lax.rem(self.group + shift, self.half)
        return pltpu.make_async_remote_copy(
            src_ref=self.far_out.at[shift, self.rows_of(c)], dst_ref=self.far_in.at[shift, self.rows_of(c)],
            send_sem=self.far_send.at[c, shift], recv_sem=self.far_recv.at[c, shift],
            device_id={"mp": target * 2 + self.parity}, device_id_type=MESH)

    def start(self, c):
        for g in range(self.half):
            self.near(c, g).start()

    def pair_sum(self, c, group):
        return self.block(c, group * 2 + self.parity)[...].astype(jnp.float32) + self.near_in[
            group, self.rows_of(c)].astype(jnp.float32)

    def send_sums(self, c):
        for g in range(self.half):
            self.near(c, g).wait_recv()
        for shift in range(1, self.half):
            target = lax.rem(self.group + shift, self.half)
            self.far_out[shift, self.rows_of(c)] = self.pair_sum(c, target).astype(jnp.bfloat16)
            self.far(c, shift).start()

    def total(self, c):
        value = self.pair_sum(c, self.group)
        for shift in range(1, self.half):
            self.far(c, shift).wait_recv()
            value = value + self.far_in[shift, self.rows_of(c)].astype(jnp.float32)
        return value

    def finish(self, c):
        for g in range(self.half):
            self.near(c, g).wait_send()
        for shift in range(1, self.half):
            self.far(c, shift).wait_send()


def reduce_scratch(rows, width, n):
    dma = pltpu.SemaphoreType.DMA((CHUNKS, n // 2))
    buffers = [pltpu.VMEM((rows, width * n), jnp.bfloat16)] + [
        pltpu.VMEM((n // 2, rows, width), jnp.bfloat16) for _ in range(3)]
    return buffers + [dma] * 4


def dot_tiles(left, right, out, rows):
    columns = out.shape[1]
    tile = min(columns, 512)

    @pl.loop(0, columns // tile)
    def _(index):
        cols = pl.ds(pl.multiple_of(index * tile, tile), tile)
        out[rows, cols] = jnp.dot(
            left[rows, :], right[:, cols], preferred_element_type=jnp.float32).astype(out.dtype)


def middle_kernel(
    n, n_mp, attn, w_out, hidden, gain, w_gate, w_up, w_down, mid_out, units, w_down_full,
    normed, mid_full, part, near_in, far_out, far_in, *sems
):
    rows, width = hidden.shape
    step = rows // CHUNKS
    piece_rows, piece_width = w_down.shape[0] // DOWN_PIECES, w_down.shape[1]
    pieces = [
        (w_down.at[pl.ds(p * piece_rows, piece_rows)],
         lambda r, p=p: w_down_full.at[
             pl.ds(p * piece_rows, piece_rows), pl.ds(pl.multiple_of(r * piece_width, piece_width), piece_width)])
        for p in range(DOWN_PIECES)
    ]
    reduce = Reduce(n_mp, part, near_in, far_out, far_in, sems[:4])
    me = reduce.me

    def mid_block(c, r):
        return mid_full.at[pl.ds(c * step, step), pl.ds(pl.multiple_of(r * width, width), width)]

    down = Gather("req", n, pieces, sems[4:9])
    spread = Gather(
        "mp", n_mp, [(mid_block(c, me), lambda r, c=c: mid_block(c, r)) for c in range(CHUNKS)],
        sems[9:13] + (None,))
    barrier = pltpu.get_barrier_semaphore()
    pl.semaphore_wait(barrier, down.greet(barrier) + spread.greet(barrier))
    for p in range(2):
        down.start(p)

    def chunk_rows(c):
        return pl.ds(c * step, step)

    def mid_chunk(c):
        value = (hidden[chunk_rows(c)].astype(jnp.float32) + reduce.total(c)).astype(jnp.bfloat16)
        mid_block(c, me)[...] = value
        mid_out[chunk_rows(c)] = value
        spread.start(c)

    for c in range(CHUNKS + 3):
        if c < CHUNKS:
            dot_tiles(attn, w_out, part, chunk_rows(c))
            reduce.start(c)
        if 1 <= c <= CHUNKS:
            reduce.send_sums(c - 1)
        if 2 <= c <= CHUNKS + 1:
            mid_chunk(c - 2)
        if 3 <= c:
            spread.forward(c - 3)
    down.forward(0)
    down.start(2)
    columns = units.shape[1]
    tile = min(columns, 512)
    for c in range(CHUNKS):
        for shift in range(spread.half):
            spread.near(c, shift).wait_recv()
        values = mid_full[chunk_rows(c)].astype(jnp.float32)
        meansq = jnp.mean(values * values, axis=-1, keepdims=True)
        normed[...] = (values * lax.rsqrt(meansq + EPSILON) * gain[...].astype(jnp.float32)).astype(jnp.bfloat16)

        @pl.loop(0, columns // tile)
        def _(index, c=c):
            cols = pl.ds(pl.multiple_of(index * tile, tile), tile)
            gate = jnp.dot(normed[...], w_gate[:, cols], preferred_element_type=jnp.float32)
            upper = jnp.dot(normed[...], w_up[:, cols], preferred_element_type=jnp.float32)
            units[chunk_rows(c), cols] = (gate * jax.nn.sigmoid(gate) * upper).astype(units.dtype)

        if c == 1:
            down.forward(1)
            down.start(3)
    for p in range(2, DOWN_PIECES):
        down.forward(p)
    for c in range(CHUNKS):
        reduce.finish(c)
        for shift in range(1, spread.half):
            spread.far(c, shift).wait_send()
        for shift in range(spread.half):
            spread.near(c, shift).wait_send()
    for p in range(DOWN_PIECES):
        down.finish(p)


def middle(n, n_mp, attn, w_out_full, hidden_in, gain, w_gate_full, w_up_full, w_down):
    rows, width = hidden_in.shape
    features = width * n_mp
    vmem, hbm = pl.BlockSpec(memory_space=pltpu.VMEM), pl.BlockSpec(memory_space=pl.ANY)
    like, bf16 = jax.ShapeDtypeStruct, jnp.bfloat16
    dma = pltpu.SemaphoreType.DMA
    return pl.pallas_call(
        functools.partial(middle_kernel, n, n_mp),
        out_shape=(
            like((rows, width), bf16),
            like((rows, w_gate_full.shape[1]), bf16),
            like((w_down.shape[0], w_down.shape[1] * n), bf16),
        ),
        in_specs=[vmem] * 6 + [hbm],
        out_specs=(vmem, vmem, hbm),
        scratch_shapes=[pltpu.VMEM((rows // CHUNKS, features), bf16), pltpu.VMEM((rows, features), bf16)]
        + reduce_scratch(rows, width, n_mp) + gather_sems(DOWN_PIECES, n)
        + [dma((CHUNKS, n_mp // 2)) for _ in range(4)],
        compiler_params=pltpu.CompilerParams(
            collective_id=2, has_side_effects=True, vmem_limit_bytes=56 * 1024 * 1024),
    )(attn, w_out_full, hidden_in, gain.reshape(1, features), w_gate_full, w_up_full, w_down)


def last_kernel(n_mp, units, w_down, mid, out, part, near_in, far_out, far_in, *sems):
    rows = mid.shape[0]
    step = rows // CHUNKS
    reduce = Reduce(n_mp, part, near_in, far_out, far_in, sems)
    barrier = pltpu.get_barrier_semaphore()
    for shift in range(1, reduce.half):
        target = lax.rem(reduce.group + shift, reduce.half) * 2 + reduce.parity
        pl.semaphore_signal(barrier, inc=1, device_id={"mp": target}, device_id_type=MESH)
    pl.semaphore_signal(barrier, inc=1, device_id={"mp": reduce.partner}, device_id_type=MESH)
    pl.semaphore_wait(barrier, reduce.half)
    for c in range(CHUNKS + 2):
        if c < CHUNKS:
            dot_tiles(units, w_down, part, pl.ds(c * step, step))
            reduce.start(c)
        if 1 <= c <= CHUNKS:
            reduce.send_sums(c - 1)
        if 2 <= c:
            chunk = pl.ds((c - 2) * step, step)
            out[chunk] = (mid[chunk].astype(jnp.float32) + reduce.total(c - 2)).astype(out.dtype)
    for c in range(CHUNKS):
        reduce.finish(c)


def last(n_mp, units, w_down_full, mid):
    rows, width = mid.shape
    vmem = pl.BlockSpec(memory_space=pltpu.VMEM)
    return pl.pallas_call(
        functools.partial(last_kernel, n_mp),
        out_shape=jax.ShapeDtypeStruct((rows, width), jnp.bfloat16),
        in_specs=[vmem] * 3,
        out_specs=vmem,
        scratch_shapes=reduce_scratch(rows, width, n_mp),
        compiler_params=pltpu.CompilerParams(
            collective_id=3, has_side_effects=True, vmem_limit_bytes=48 * 1024 * 1024),
    )(units, w_down_full, mid)


def on_device(
    n, n_mp, hidden_in, w_qkv, w_out, attn_gain, mlp_gain, w_gate, w_up, w_down, k_cache, v_cache, cache_len
):
    new_count = hidden_in.shape[0]
    width = w_qkv.shape[2]
    heads_local = width // HD
    full_rows, w_qkv_full = gather_first(n, n_mp, hidden_in, w_qkv)
    normed = rms_scale(full_rows, attn_gain)
    columns = normed
    projected = jnp.einsum(
        "nd,kdw->knw",
        columns,
        w_qkv_full,
        preferred_element_type=jnp.float32,
    )
    length = cache_len[0]
    positions = (length + jnp.arange(new_count, dtype=jnp.int32)).astype(jnp.float32)
    queries = rotate(projected[0].reshape(new_count, heads_local, HD), positions).astype(
        jnp.bfloat16
    )
    fresh_keys = rotate(projected[1].reshape(new_count, heads_local, HD), positions).astype(
        jnp.bfloat16
    )
    fresh_values = projected[2].astype(jnp.bfloat16).reshape(new_count, heads_local, HD)
    attn, w_out_full, w_gate_full, w_up_full = attend_and_gather(
        n, cache_len, queries.reshape(new_count, width), fresh_keys.reshape(new_count, width),
        fresh_values.reshape(new_count, width), k_cache, v_cache, w_out, w_gate, w_up)
    mid_local, units, w_down_full = middle(
        n, n_mp, attn, w_out_full, hidden_in, mlp_gain, w_gate_full, w_up_full, w_down)
    hidden_out = last(n_mp, units, w_down_full, mid_local)
    return (
        hidden_out,
        fresh_keys.reshape(new_count, width),
        fresh_values.reshape(new_count, width),
    )


def solution(mesh):
    return jax.shard_map(
        functools.partial(on_device, mesh.shape["req"], mesh.shape["mp"]),
        mesh=mesh,
        in_specs=(
            P("req", "mp"),
            P(None, "req", "mp"),
            P("mp", "req"),
            P(),
            P(),
            P("req", "mp"),
            P("req", "mp"),
            P("mp", "req"),
            P("req", None, "mp"),
            P("req", None, "mp"),
            P("req"),
        ),
        out_specs=(P("req", "mp"), P("req", "mp"), P("req", "mp")),
        check_vma=False,
    )
```

```python
import functools

import jax
import jax.numpy as jnp
from jax import lax
from jax.experimental import pallas as pl
from jax.experimental.pallas import tpu as pltpu
from jax.sharding import PartitionSpec as P

HD = 64
MESH = pl.DeviceIdType.MESH
LOG2E = 1.4426950408889634
PAIR = 2 * HD

THETA = 130000.0
EPSILON = 1e-05
NEG_FILL = -1e30


def rotation(positions):
    half = HD // 2
    freq = THETA ** (-(jnp.arange(half, dtype=jnp.float32) * 2.0 / HD))
    angle = positions[:, None] * freq[None, :]
    cosine, sine = jnp.cos(angle), jnp.sin(angle)
    return jnp.tile(cosine, (1, 4)), jnp.tile(jnp.concatenate([-sine, sine], axis=1), (1, 2))


def columns_of(ref, index, width):
    return ref.at[:, pl.ds(pl.multiple_of(index * width, width), width)]


class Gather:
    def __init__(self, axis, n, pieces, sems):
        self.axis = axis
        self.half = n // 2
        self.pieces = pieces
        self.send_far, self.recv_far, self.send_near, self.recv_near, self.own_sem = sems
        me = lax.axis_index(axis)
        self.group, self.parity = me // 2, lax.rem(me, 2)
        self.me, self.partner = me, me + 1 - 2 * self.parity

    def member(self, shift):
        return lax.rem(self.group + shift + self.half, self.half) * 2 + self.parity

    def greet(self, barrier):
        for shift in range(1, self.half):
            pl.semaphore_signal(barrier, inc=1, device_id={self.axis: self.member(shift)}, device_id_type=MESH)
        pl.semaphore_signal(barrier, inc=1, device_id={self.axis: self.partner}, device_id_type=MESH)
        return self.half

    def far(self, c, shift):
        src, slot = self.pieces[c]
        return pltpu.make_async_remote_copy(
            src_ref=src, dst_ref=slot(self.me), send_sem=self.send_far.at[c, shift],
            recv_sem=self.recv_far.at[c, shift], device_id={self.axis: self.member(shift)}, device_id_type=MESH)

    def near(self, c, shift):
        src, slot = self.pieces[c]
        owner = self.member(-shift)
        return pltpu.make_async_remote_copy(
            src_ref=src if shift == 0 else slot(owner), dst_ref=slot(owner), send_sem=self.send_near.at[c, shift],
            recv_sem=self.recv_near.at[c, shift], device_id={self.axis: self.partner}, device_id_type=MESH)

    def own(self, c):
        src, slot = self.pieces[c]
        return pltpu.make_async_copy(src, slot(self.me), self.own_sem.at[c])

    def start(self, c):
        for shift in range(1, self.half):
            self.far(c, shift).start()
        self.near(c, 0).start()
        if self.own_sem is not None:
            self.own(c).start()

    def forward(self, c):
        for shift in range(1, self.half):
            self.far(c, shift).wait_recv()
            self.near(c, shift).start()

    def finish(self, c):
        for shift in range(1, self.half):
            self.far(c, shift).wait_send()
        for shift in range(self.half):
            self.near(c, shift).wait()
        if self.own_sem is not None:
            self.own(c).wait()


def gather_sems(pieces, n):
    dma = pltpu.SemaphoreType.DMA
    return [dma((pieces, n // 2)) for _ in range(4)] + [dma((pieces,))]


def first_kernel(n, n_mp, hid, wqkv, hid_full, wqkv_full, *sems):
    mp_send, mp_recv, mp_own = sems[5:]
    depth, width = wqkv.shape[1], hid.shape[1]
    rows = depth // 2
    pieces = [
        (wqkv.at[i, pl.ds(part * rows, rows)],
         lambda r, i=i, part=part: wqkv_full.at[
             i, pl.ds(pl.multiple_of(r * depth + part * rows, rows), rows)])
        for i in range(3) for part in range(2)
    ]
    gather = Gather("req", n, pieces, sems[:5])
    me = lax.axis_index("mp")
    barrier = pltpu.get_barrier_semaphore()
    expected = gather.greet(barrier)
    for shift in range(1, n_mp):
        pl.semaphore_signal(barrier, inc=1, device_id={"mp": lax.rem(me + shift, n_mp)}, device_id_type=MESH)
    pl.semaphore_wait(barrier, expected + n_mp - 1)
    mine = columns_of(hid_full, me, width)
    copies = [
        pltpu.make_async_remote_copy(
            src_ref=hid, dst_ref=mine, send_sem=mp_send.at[shift], recv_sem=mp_recv.at[shift],
            device_id={"mp": lax.rem(me + shift, n_mp)}, device_id_type=MESH)
        for shift in range(1, n_mp)
    ]
    own = pltpu.make_async_copy(hid, mine, mp_own)
    for c in range(6):
        gather.start(c)
    for copy in copies:
        copy.start()
    own.start()
    for c in range(6):
        gather.forward(c)
    for c in range(6):
        gather.finish(c)
    for copy in copies:
        copy.wait()
    own.wait()


def gather_first(n, n_mp, hidden_in, w_qkv):
    rows, width = hidden_in.shape
    dma = pltpu.SemaphoreType.DMA
    hbm = pl.BlockSpec(memory_space=pl.ANY)
    return pl.pallas_call(
        functools.partial(first_kernel, n, n_mp),
        out_shape=(
            jax.ShapeDtypeStruct((rows, width * n_mp), hidden_in.dtype),
            jax.ShapeDtypeStruct((3, w_qkv.shape[1] * n, w_qkv.shape[2]), w_qkv.dtype),
        ),
        in_specs=[hbm, hbm],
        out_specs=(hbm, hbm),
        scratch_shapes=gather_sems(6, n) + [dma((n_mp,)), dma((n_mp,)), dma],
        compiler_params=pltpu.CompilerParams(collective_id=0, has_side_effects=True),
    )(hidden_in, w_qkv)


def project(hidden, gain, w_qkv, cosine, sine, queries, keys, values):
    rows, width = queries.shape
    step = min(rows, 256)
    lane = lax.broadcasted_iota(jnp.int32, (1, PAIR), 1)
    first = lax.rem(lane, HD) < HD // 2

    @pl.loop(0, rows // step)
    def _(index):
        chunk = pl.ds(pl.multiple_of(index * step, step), step)
        entries = hidden[chunk, :].astype(jnp.float32)
        meansq = jnp.mean(entries * entries, axis=-1, keepdims=True)
        normed = (entries * lax.rsqrt(meansq + EPSILON) * gain[...].astype(jnp.float32)).astype(jnp.bfloat16)
        for i, out in enumerate((queries, keys, values)):
            product = jnp.dot(normed, w_qkv[i], preferred_element_type=jnp.float32)
            for begin in range(0, width, PAIR):
                part = product[:, begin : begin + PAIR]
                if i < 2:
                    other = jnp.where(first, pltpu.roll(part, PAIR - HD // 2, 1), pltpu.roll(part, HD // 2, 1))
                    part = part * cosine[chunk, :] + other * sine[chunk, :]
                out[chunk, begin : begin + PAIR] = part.astype(out.dtype)


def attend(length, pair, q_begin, rows, q_ref, kn_ref, vn_ref, kc_ref, vc_ref, out_ref):
    fresh = kn_ref.shape[0]
    slots = kc_ref.shape[1]
    block = min(slots, 512)
    lane = lax.broadcasted_iota(jnp.int32, (1, PAIR), 1)
    masks = (lane < HD, lane >= HD)
    cols = pl.ds(pl.multiple_of(pair * PAIR, PAIR), PAIR)
    query = q_ref[pl.ds(pl.multiple_of(q_begin, rows), rows), cols]
    queries = [jnp.where(mask, query, 0) for mask in masks]
    row_index = q_begin + lax.broadcasted_iota(jnp.int32, (rows, 1), 0)

    def absorb(state, keys, values, hide):
        out = []
        for mask, mine, (top, accum) in zip(masks, queries, state):
            scores = lax.dot_general(
                mine, keys, (((1,), (1,)), ((), ())), preferred_element_type=jnp.float32)
            scores = hide(scores * (LOG2E * HD**-0.5))
            new_top = jnp.maximum(top, jnp.max(scores, axis=1, keepdims=True))
            probs = jnp.exp2(scores - new_top).astype(jnp.bfloat16)
            extended = jnp.where(mask, values, 1)
            accum = accum * jnp.exp2(top - new_top) + jnp.dot(
                probs, extended, preferred_element_type=jnp.float32)
            out.append((new_top, accum))
        return tuple(out)

    state = tuple(
        (jnp.full((rows, 1), NEG_FILL, jnp.float32), jnp.zeros((rows, PAIR), jnp.float32)) for _ in masks)

    def fresh_step(index, state):
        begin = pl.multiple_of(index * block, block)
        column = begin + lax.broadcasted_iota(jnp.int32, (1, block), 1)
        return absorb(
            state, kn_ref[pl.ds(begin, block), cols], vn_ref[pl.ds(begin, block), cols],
            lambda scores: jnp.where(row_index >= column, scores, NEG_FILL))

    def cache_step(index, state):
        begin = pl.multiple_of(index * block, block)
        column = begin + lax.broadcasted_iota(jnp.int32, (1, block), 1)
        bias = jnp.where(column < length, 0.0, NEG_FILL)
        return absorb(
            state, kc_ref[0, pl.ds(begin, block)], vc_ref[0, pl.ds(begin, block)],
            lambda scores: scores + bias)

    state = lax.fori_loop(0, fresh // block, fresh_step, state)
    state = lax.fori_loop(0, slots // block, cache_step, state)
    parts = [accum / pltpu.roll(accum, HD, 1) for _, accum in state]
    out_ref[...] = jnp.where(masks[0], parts[0], parts[1]).astype(out_ref.dtype)


QUARTERS = 4
PIECES = 1 + 2 * QUARTERS


def attention_kernel(
    n, n_pairs, n_blocks, length_ref, hidden, gain, w_qkv, cosine, sine, kc_ref, vc_ref, w_out, w_gate, w_up,
    out_ref, keys, values, w_out_full, w_gate_full, w_up_full, queries, *sems
):
    step = pl.program_id(0) * n_blocks + pl.program_id(1)
    steps = n_pairs * n_blocks
    pieces = [(w_out, lambda r: columns_of(w_out_full, r, w_out.shape[1]))]
    for src, full in ((w_gate, w_gate_full), (w_up, w_up_full)):
        depth = src.shape[0]
        for part in range(QUARTERS):
            rows = depth // QUARTERS
            pieces.append((
                src.at[pl.ds(part * rows, rows)],
                lambda r, full=full, part=part, depth=depth, rows=rows: full.at[
                    pl.ds(pl.multiple_of(r * depth + part * rows, rows), rows)]))
    gather = Gather("req", n, pieces, sems)

    @pl.when(step == 0)
    def _():
        barrier = pltpu.get_barrier_semaphore()
        pl.semaphore_wait(barrier, gather.greet(barrier))
        for c in range(PIECES):
            gather.start(c)
        project(hidden, gain, w_qkv, cosine, sine, queries, keys, values)

    rows = out_ref.shape[0]
    attend(
        length_ref[0], pl.program_id(0), pl.program_id(1) * rows, rows, queries, keys, values, kc_ref, vc_ref,
        out_ref)

    for c in range(PIECES):
        @pl.when(step == min(c, steps - 1))
        def _(c=c):
            gather.forward(c)

    @pl.when(step == steps - 1)
    def _():
        for c in range(PIECES):
            gather.finish(c)


def attend_and_gather(n, length, hidden, gain, w_qkv, cosine, sine, k_cache, v_cache, w_out, w_gate, w_up):
    rows, features = hidden.shape
    width = w_qkv.shape[2]
    slots = k_cache.shape[1]
    n_pairs, n_blocks = width // PAIR, 2
    hbm = pl.BlockSpec(memory_space=pl.ANY)
    row_block = pl.BlockSpec((rows // n_blocks, PAIR), lambda h, i: (i, h))
    cached = pl.BlockSpec((1, slots, PAIR), lambda h, i: (0, 0, h))

    def whole(*shape):
        return pl.BlockSpec(shape, lambda h, i: (0,) * len(shape), pipeline_mode=pl.Buffered(1))

    fresh = pl.BlockSpec((rows, width), lambda h, i: (0, 0))
    like, bf16 = jax.ShapeDtypeStruct, jnp.bfloat16
    return pl.pallas_call(
        functools.partial(attention_kernel, n, n_pairs, n_blocks),
        grid=(n_pairs, n_blocks),
        out_shape=(
            like((rows, width), bf16),
            like((rows, width), bf16),
            like((rows, width), bf16),
            like((w_out.shape[0], w_out.shape[1] * n), w_out.dtype),
            like((w_gate.shape[0] * n, w_gate.shape[1]), w_gate.dtype),
            like((w_up.shape[0] * n, w_up.shape[1]), w_up.dtype),
        ),
        in_specs=[
            pl.BlockSpec(memory_space=pltpu.SMEM), whole(rows, features), whole(1, features),
            whole(*w_qkv.shape), whole(rows, PAIR), whole(rows, PAIR), cached, cached,
        ] + [hbm] * 3,
        out_specs=(row_block, fresh, fresh) + (hbm,) * 3,
        scratch_shapes=[pltpu.VMEM((rows, width), bf16)] + gather_sems(PIECES, n),
        compiler_params=pltpu.CompilerParams(
            collective_id=1, has_side_effects=True, vmem_limit_bytes=56 * 1024 * 1024,
            dimension_semantics=("arbitrary", "arbitrary")),
    )(length, hidden, gain.reshape(1, features), w_qkv, cosine, sine, k_cache, v_cache, w_out, w_gate, w_up)


CHUNKS = 4
DOWN_PIECES = 8


class Reduce:
    def __init__(self, n, part, near_in, far_out, far_in, sems):
        self.half, self.part, self.near_in, self.far_out, self.far_in = n // 2, part, near_in, far_out, far_in
        self.near_send, self.near_recv, self.far_send, self.far_recv = sems
        self.me = lax.axis_index("mp")
        self.group, self.parity = self.me // 2, lax.rem(self.me, 2)
        self.partner = self.me + 1 - 2 * self.parity
        self.width = part.shape[1] // n
        self.rows = part.shape[0] // CHUNKS

    def rows_of(self, c):
        return pl.ds(c * self.rows, self.rows)

    def block(self, c, index):
        return self.part.at[
            self.rows_of(c), pl.ds(pl.multiple_of(index * self.width, self.width), self.width)]

    def near(self, c, g):
        return pltpu.make_async_remote_copy(
            src_ref=self.block(c, g * 2 + 1 - self.parity), dst_ref=self.near_in.at[g, self.rows_of(c)],
            send_sem=self.near_send.at[c, g], recv_sem=self.near_recv.at[c, g],
            device_id={"mp": self.partner}, device_id_type=MESH)

    def far(self, c, shift):
        target = lax.rem(self.group + shift, self.half)
        return pltpu.make_async_remote_copy(
            src_ref=self.far_out.at[shift, self.rows_of(c)], dst_ref=self.far_in.at[shift, self.rows_of(c)],
            send_sem=self.far_send.at[c, shift], recv_sem=self.far_recv.at[c, shift],
            device_id={"mp": target * 2 + self.parity}, device_id_type=MESH)

    def start(self, c):
        for g in range(self.half):
            self.near(c, g).start()

    def pair_sum(self, c, group):
        return self.block(c, group * 2 + self.parity)[...].astype(jnp.float32) + self.near_in[
            group, self.rows_of(c)].astype(jnp.float32)

    def send_sums(self, c):
        for g in range(self.half):
            self.near(c, g).wait_recv()
        for shift in range(1, self.half):
            target = lax.rem(self.group + shift, self.half)
            self.far_out[shift, self.rows_of(c)] = self.pair_sum(c, target).astype(jnp.bfloat16)
            self.far(c, shift).start()

    def total(self, c):
        value = self.pair_sum(c, self.group)
        for shift in range(1, self.half):
            self.far(c, shift).wait_recv()
            value = value + self.far_in[shift, self.rows_of(c)].astype(jnp.float32)
        return value

    def finish(self, c):
        for g in range(self.half):
            self.near(c, g).wait_send()
        for shift in range(1, self.half):
            self.far(c, shift).wait_send()


def reduce_scratch(rows, width, n):
    dma = pltpu.SemaphoreType.DMA((CHUNKS, n // 2))
    buffers = [pltpu.VMEM((rows, width * n), jnp.bfloat16)] + [
        pltpu.VMEM((n // 2, rows, width), jnp.bfloat16) for _ in range(3)]
    return buffers + [dma] * 4


def dot_tiles(left, right, out, rows):
    columns = out.shape[1]
    tile = min(columns, 512)

    @pl.loop(0, columns // tile)
    def _(index):
        cols = pl.ds(pl.multiple_of(index * tile, tile), tile)
        out[rows, cols] = jnp.dot(
            left[rows, :], right[:, cols], preferred_element_type=jnp.float32).astype(out.dtype)


def middle_kernel(
    n, n_mp, attn, w_out, hidden, gain, w_gate_full, w_up_full, w_down, mid_out, units, w_down_full,
    gate_in, up_in, load_sems, normed, mid_full, part, near_in, far_out, far_in, *sems
):
    rows, width = hidden.shape
    step = rows // CHUNKS
    piece_rows, piece_width = w_down.shape[0] // DOWN_PIECES, w_down.shape[1]
    pieces = [
        (w_down.at[pl.ds(p * piece_rows, piece_rows)],
         lambda r, p=p: w_down_full.at[
             pl.ds(p * piece_rows, piece_rows), pl.ds(pl.multiple_of(r * piece_width, piece_width), piece_width)])
        for p in range(DOWN_PIECES)
    ]
    reduce = Reduce(n_mp, part, near_in, far_out, far_in, sems[:4])
    me = reduce.me

    def mid_block(c, r):
        return mid_full.at[pl.ds(c * step, step), pl.ds(pl.multiple_of(r * width, width), width)]

    down = Gather("req", n, pieces, sems[4:9])
    spread = Gather(
        "mp", n_mp, [(mid_block(c, me), lambda r, c=c: mid_block(c, r)) for c in range(CHUNKS)],
        sems[9:13] + (None,))
    barrier = pltpu.get_barrier_semaphore()
    pl.semaphore_wait(barrier, down.greet(barrier) + spread.greet(barrier))
    for p in range(DOWN_PIECES):
        down.start(p)
    loads = [
        pltpu.make_async_copy(w_gate_full, gate_in, load_sems.at[0]),
        pltpu.make_async_copy(w_up_full, up_in, load_sems.at[1]),
    ]
    for load in loads:
        load.start()

    def chunk_rows(c):
        return pl.ds(c * step, step)

    def mid_chunk(c):
        value = (hidden[chunk_rows(c)].astype(jnp.float32) + reduce.total(c)).astype(jnp.bfloat16)
        mid_block(c, me)[...] = value
        mid_out[chunk_rows(c)] = value
        spread.start(c)

    for c in range(CHUNKS + 3):
        if c < CHUNKS:
            dot_tiles(attn, w_out, part, chunk_rows(c))
            reduce.start(c)
        if 1 <= c <= CHUNKS:
            reduce.send_sums(c - 1)
        if 2 <= c <= CHUNKS + 1:
            mid_chunk(c - 2)
        if 3 <= c:
            spread.forward(c - 3)
        if 2 <= c:
            down.forward(c - 2)
    for load in loads:
        load.wait()
    columns = units.shape[1]
    tile = min(columns, 512)
    for c in range(CHUNKS):
        for shift in range(spread.half):
            spread.near(c, shift).wait_recv()
        values = mid_full[chunk_rows(c)].astype(jnp.float32)
        meansq = jnp.mean(values * values, axis=-1, keepdims=True)
        normed[...] = (values * lax.rsqrt(meansq + EPSILON) * gain[...].astype(jnp.float32)).astype(jnp.bfloat16)

        @pl.loop(0, columns // tile)
        def _(index, c=c):
            cols = pl.ds(pl.multiple_of(index * tile, tile), tile)
            gate = jnp.dot(normed[...], gate_in[:, cols], preferred_element_type=jnp.float32)
            upper = jnp.dot(normed[...], up_in[:, cols], preferred_element_type=jnp.float32)
            units[chunk_rows(c), cols] = (gate * jax.nn.sigmoid(gate) * upper).astype(units.dtype)

        if CHUNKS + 1 + c < DOWN_PIECES:
            down.forward(CHUNKS + 1 + c)
    for c in range(CHUNKS):
        reduce.finish(c)
        for shift in range(1, spread.half):
            spread.far(c, shift).wait_send()
        for shift in range(spread.half):
            spread.near(c, shift).wait_send()
    for p in range(DOWN_PIECES):
        down.finish(p)


def middle(n, n_mp, attn, w_out_full, hidden_in, gain, w_gate_full, w_up_full, w_down):
    rows, width = hidden_in.shape
    features = width * n_mp
    vmem, hbm = pl.BlockSpec(memory_space=pltpu.VMEM), pl.BlockSpec(memory_space=pl.ANY)
    like, bf16 = jax.ShapeDtypeStruct, jnp.bfloat16
    dma = pltpu.SemaphoreType.DMA
    return pl.pallas_call(
        functools.partial(middle_kernel, n, n_mp),
        out_shape=(
            like((rows, width), bf16),
            like((rows, w_gate_full.shape[1]), bf16),
            like((w_down.shape[0], w_down.shape[1] * n), bf16),
        ),
        in_specs=[vmem] * 4 + [hbm] * 3,
        out_specs=(vmem, vmem, hbm),
        scratch_shapes=[pltpu.VMEM(w_gate_full.shape, bf16), pltpu.VMEM(w_up_full.shape, bf16), dma((2,))]
        + [pltpu.VMEM((rows // CHUNKS, features), bf16), pltpu.VMEM((rows, features), bf16)]
        + reduce_scratch(rows, width, n_mp) + gather_sems(DOWN_PIECES, n)
        + [dma((CHUNKS, n_mp // 2)) for _ in range(4)],
        compiler_params=pltpu.CompilerParams(
            collective_id=2, has_side_effects=True, vmem_limit_bytes=56 * 1024 * 1024),
    )(attn, w_out_full, hidden_in, gain.reshape(1, features), w_gate_full, w_up_full, w_down)


def last_kernel(n_mp, units, w_down, mid, out, part, near_in, far_out, far_in, *sems):
    rows = mid.shape[0]
    step = rows // CHUNKS
    reduce = Reduce(n_mp, part, near_in, far_out, far_in, sems)
    barrier = pltpu.get_barrier_semaphore()
    for shift in range(1, reduce.half):
        target = lax.rem(reduce.group + shift, reduce.half) * 2 + reduce.parity
        pl.semaphore_signal(barrier, inc=1, device_id={"mp": target}, device_id_type=MESH)
    pl.semaphore_signal(barrier, inc=1, device_id={"mp": reduce.partner}, device_id_type=MESH)
    pl.semaphore_wait(barrier, reduce.half)
    for c in range(CHUNKS + 2):
        if c < CHUNKS:
            dot_tiles(units, w_down, part, pl.ds(c * step, step))
            reduce.start(c)
        if 1 <= c <= CHUNKS:
            reduce.send_sums(c - 1)
        if 2 <= c:
            chunk = pl.ds((c - 2) * step, step)
            out[chunk] = (mid[chunk].astype(jnp.float32) + reduce.total(c - 2)).astype(out.dtype)
    for c in range(CHUNKS):
        reduce.finish(c)


def last(n_mp, units, w_down_full, mid):
    rows, width = mid.shape
    vmem = pl.BlockSpec(memory_space=pltpu.VMEM)
    return pl.pallas_call(
        functools.partial(last_kernel, n_mp),
        out_shape=jax.ShapeDtypeStruct((rows, width), jnp.bfloat16),
        in_specs=[vmem] * 3,
        out_specs=vmem,
        scratch_shapes=reduce_scratch(rows, width, n_mp),
        compiler_params=pltpu.CompilerParams(
            collective_id=3, has_side_effects=True, vmem_limit_bytes=48 * 1024 * 1024),
    )(units, w_down_full, mid)


def on_device(
    n, n_mp, hidden_in, w_qkv, w_out, attn_gain, mlp_gain, w_gate, w_up, w_down, k_cache, v_cache, cache_len
):
    new_count = hidden_in.shape[0]
    full_rows, w_qkv_full = gather_first(n, n_mp, hidden_in, w_qkv)
    positions = (cache_len[0] + jnp.arange(new_count, dtype=jnp.int32)).astype(jnp.float32)
    cosine, sine = rotation(positions)
    attn, fresh_keys, fresh_values, w_out_full, w_gate_full, w_up_full = attend_and_gather(
        n, cache_len, full_rows, attn_gain, w_qkv_full, cosine, sine, k_cache, v_cache, w_out, w_gate, w_up)
    mid_local, units, w_down_full = middle(
        n, n_mp, attn, w_out_full, hidden_in, mlp_gain, w_gate_full, w_up_full, w_down)
    hidden_out = last(n_mp, units, w_down_full, mid_local)
    return hidden_out, fresh_keys, fresh_values


def solution(mesh):
    return jax.shard_map(
        functools.partial(on_device, mesh.shape["req"], mesh.shape["mp"]),
        mesh=mesh,
        in_specs=(
            P("req", "mp"),
            P(None, "req", "mp"),
            P("mp", "req"),
            P(),
            P(),
            P("req", "mp"),
            P("req", "mp"),
            P("mp", "req"),
            P("req", None, "mp"),
            P("req", None, "mp"),
            P("req"),
        ),
        out_specs=(P("req", "mp"), P("req", "mp"), P("req", "mp")),
        check_vma=False,
    )
```

```python
import functools

import jax
import jax.numpy as jnp
from jax import lax
from jax.experimental import pallas as pl
from jax.experimental.pallas import tpu as pltpu
from jax.sharding import PartitionSpec as P

HD = 64
MESH = pl.DeviceIdType.MESH
LOG2E = 1.4426950408889634
PAIR = 2 * HD

THETA = 130000.0
EPSILON = 1e-05
NEG_FILL = -1e30


def rotation(positions):
    half = HD // 2
    freq = THETA ** (-(jnp.arange(half, dtype=jnp.float32) * 2.0 / HD))
    angle = positions[:, None] * freq[None, :]
    cosine, sine = jnp.cos(angle), jnp.sin(angle)
    return jnp.tile(cosine, (1, 4)), jnp.tile(jnp.concatenate([-sine, sine], axis=1), (1, 2))


def columns_of(ref, index, width):
    return ref.at[:, pl.ds(pl.multiple_of(index * width, width), width)]


class Gather:
    def __init__(self, axis, n, pieces, sems):
        self.axis = axis
        self.half = n // 2
        self.pieces = pieces
        self.send_far, self.recv_far, self.send_near, self.recv_near, self.own_sem = sems
        me = lax.axis_index(axis)
        self.group, self.parity = me // 2, lax.rem(me, 2)
        self.me, self.partner = me, me + 1 - 2 * self.parity

    def member(self, shift):
        return lax.rem(self.group + shift + self.half, self.half) * 2 + self.parity

    def greet(self, barrier):
        for shift in range(1, self.half):
            pl.semaphore_signal(barrier, inc=1, device_id={self.axis: self.member(shift)}, device_id_type=MESH)
        pl.semaphore_signal(barrier, inc=1, device_id={self.axis: self.partner}, device_id_type=MESH)
        return self.half

    def far(self, c, shift):
        src, slot = self.pieces[c]
        return pltpu.make_async_remote_copy(
            src_ref=src, dst_ref=slot(self.me), send_sem=self.send_far.at[c, shift],
            recv_sem=self.recv_far.at[c, shift], device_id={self.axis: self.member(shift)}, device_id_type=MESH)

    def near(self, c, shift):
        src, slot = self.pieces[c]
        owner = self.member(-shift)
        return pltpu.make_async_remote_copy(
            src_ref=src if shift == 0 else slot(owner), dst_ref=slot(owner), send_sem=self.send_near.at[c, shift],
            recv_sem=self.recv_near.at[c, shift], device_id={self.axis: self.partner}, device_id_type=MESH)

    def own(self, c):
        src, slot = self.pieces[c]
        return pltpu.make_async_copy(src, slot(self.me), self.own_sem.at[c])

    def start(self, c):
        for shift in range(1, self.half):
            self.far(c, shift).start()
        self.near(c, 0).start()
        if self.own_sem is not None:
            self.own(c).start()

    def forward(self, c):
        for shift in range(1, self.half):
            self.far(c, shift).wait_recv()
            self.near(c, shift).start()

    def finish(self, c):
        for shift in range(1, self.half):
            self.far(c, shift).wait_send()
        for shift in range(self.half):
            self.near(c, shift).wait()
        if self.own_sem is not None:
            self.own(c).wait()


class Chain:
    def __init__(self, n, pieces, sems):
        self.half = n // 2
        self.pieces = pieces
        self.send_far, self.recv_far, self.send_near, self.recv_near, self.own_sem = sems
        self.me = lax.axis_index("req")
        self.group, self.parity = self.me // 2, lax.rem(self.me, 2)
        self.partner = self.me + 1 - 2 * self.parity
        self.ticks = len(pieces) + self.half

    def greet(self, barrier):
        for shift in range(1, self.half):
            other = lax.rem(self.group + shift, self.half) * 2 + self.parity
            pl.semaphore_signal(barrier, inc=1, device_id={"req": other}, device_id_type=MESH)
        pl.semaphore_signal(barrier, inc=1, device_id={"req": self.partner}, device_id_type=MESH)
        return self.half

    def shards(self, c):
        return (0, 1) if c == 0 else (0,)

    def within(self, group):
        return (group >= 0) & (group < self.half)

    def owner(self, way, hop, b):
        side = self.parity if b == 0 else 1 - self.parity
        return (self.group - way * hop) * 2 + side

    def far(self, c, way, hop, b, arriving=False):
        src, slot = self.pieces[c]
        place = slot(self.owner(way, hop if arriving else hop - 1, b))
        index = ((way + 1) // 2 * self.half + hop) * 2 + b
        return pltpu.make_async_remote_copy(
            src_ref=src if hop == 1 and b == 0 and not arriving else place, dst_ref=place,
            send_sem=self.send_far.at[c, index], recv_sem=self.recv_far.at[c, index],
            device_id={"req": (self.group + way) * 2 + self.parity}, device_id_type=MESH)

    def near(self, c, way, hop):
        src, slot = self.pieces[c]
        place = slot(self.owner(way, hop, 0))
        index = (way + 1) // 2 * self.half + hop
        return pltpu.make_async_remote_copy(
            src_ref=src if hop == 0 else place, dst_ref=place, send_sem=self.send_near.at[c, index],
            recv_sem=self.recv_near.at[c, index], device_id={"req": self.partner}, device_id_type=MESH)

    def own(self, c):
        src, slot = self.pieces[c]
        return pltpu.make_async_copy(src, slot(self.me), self.own_sem.at[c])

    def send(self, c, hop):
        for way in (-1, 1):
            @pl.when(self.within(self.group + way) & self.within(self.group - way * (hop - 1)))
            def _(way=way):
                for b in self.shards(c):
                    self.far(c, way, hop, b).start()

    def start(self):
        for c in range(len(self.pieces)):
            self.near(c, 1, 0).start()
            self.own(c).start()
            if c > 0:
                self.send(c, 1)

    def relay(self, c, hop):
        for way in (-1, 1):
            @pl.when(self.within(self.group - way * hop))
            def _(way=way):
                for b in self.shards(c):
                    self.far(c, way, hop, b, arriving=True).wait_recv()
                if c > 0:
                    self.near(c, way, hop).start()
        if hop < self.half - 1:
            self.send(c, hop + 1)

    def tick(self, t):
        for c in range(len(self.pieces)):
            hop = t - c + (c > 0)
            if c == 0 and hop == 0:
                self.near(0, 1, 0).wait_recv()
                self.send(0, 1)
            elif 1 <= hop < self.half:
                self.relay(c, hop)

    def finish(self):
        for c in range(len(self.pieces)):
            self.near(c, 1, 0).wait_send()
            if c > 0:
                self.near(c, 1, 0).wait_recv()
            self.own(c).wait()
            for hop in range(1, self.half):
                for way in (-1, 1):
                    @pl.when(self.within(self.group + way) & self.within(self.group - way * (hop - 1)))
                    def _(way=way, hop=hop, c=c):
                        for b in self.shards(c):
                            self.far(c, way, hop, b).wait_send()

                    if c > 0:
                        @pl.when(self.within(self.group - way * hop))
                        def _(way=way, hop=hop, c=c):
                            self.near(c, way, hop).wait()


def gather_sems(pieces, n):
    dma = pltpu.SemaphoreType.DMA
    return [dma((pieces, 2 * n)) for _ in range(2)] + [dma((pieces, n)) for _ in range(2)] + [dma((pieces,))]


def first_kernel(n, n_mp, hid, wqkv, hid_full, wqkv_full, *sems):
    mp_send, mp_recv, mp_own = sems[5:]
    depth, width = wqkv.shape[1], hid.shape[1]
    rows = depth // 2
    pieces = [
        (wqkv.at[i, pl.ds(part * rows, rows)],
         lambda r, i=i, part=part: wqkv_full.at[
             i, pl.ds(pl.multiple_of(r * depth + part * rows, rows), rows)])
        for i in range(3) for part in range(2)
    ]
    gather = Chain(n, pieces, sems[:5])
    me = lax.axis_index("mp")
    barrier = pltpu.get_barrier_semaphore()
    expected = gather.greet(barrier)
    for shift in range(1, n_mp):
        pl.semaphore_signal(barrier, inc=1, device_id={"mp": lax.rem(me + shift, n_mp)}, device_id_type=MESH)
    pl.semaphore_wait(barrier, expected + n_mp - 1)
    mine = columns_of(hid_full, me, width)
    copies = [
        pltpu.make_async_remote_copy(
            src_ref=hid, dst_ref=mine, send_sem=mp_send.at[shift], recv_sem=mp_recv.at[shift],
            device_id={"mp": lax.rem(me + shift, n_mp)}, device_id_type=MESH)
        for shift in range(1, n_mp)
    ]
    own = pltpu.make_async_copy(hid, mine, mp_own)
    for copy in copies:
        copy.start()
    own.start()
    gather.start()
    for t in range(gather.ticks):
        gather.tick(t)
    gather.finish()
    for copy in copies:
        copy.wait()
    own.wait()


def gather_first(n, n_mp, hidden_in, w_qkv):
    rows, width = hidden_in.shape
    dma = pltpu.SemaphoreType.DMA
    hbm = pl.BlockSpec(memory_space=pl.ANY)
    return pl.pallas_call(
        functools.partial(first_kernel, n, n_mp),
        out_shape=(
            jax.ShapeDtypeStruct((rows, width * n_mp), hidden_in.dtype),
            jax.ShapeDtypeStruct((3, w_qkv.shape[1] * n, w_qkv.shape[2]), w_qkv.dtype),
        ),
        in_specs=[hbm, hbm],
        out_specs=(hbm, hbm),
        scratch_shapes=gather_sems(6, n) + [dma((n_mp,)), dma((n_mp,)), dma],
        compiler_params=pltpu.CompilerParams(collective_id=0, has_side_effects=True),
    )(hidden_in, w_qkv)


def project(hidden, gain, w_qkv, cosine, sine, queries, keys, values):
    rows, width = queries.shape
    step = min(rows, 256)
    lane = lax.broadcasted_iota(jnp.int32, (1, PAIR), 1)
    first = lax.rem(lane, HD) < HD // 2

    @pl.loop(0, rows // step)
    def _(index):
        chunk = pl.ds(pl.multiple_of(index * step, step), step)
        entries = hidden[chunk, :].astype(jnp.float32)
        meansq = jnp.mean(entries * entries, axis=-1, keepdims=True)
        normed = (entries * lax.rsqrt(meansq + EPSILON) * gain[...].astype(jnp.float32)).astype(jnp.bfloat16)
        for i, out in enumerate((queries, keys, values)):
            product = jnp.dot(normed, w_qkv[i], preferred_element_type=jnp.float32)
            for begin in range(0, width, PAIR):
                part = product[:, begin : begin + PAIR]
                if i < 2:
                    other = jnp.where(first, pltpu.roll(part, PAIR - HD // 2, 1), pltpu.roll(part, HD // 2, 1))
                    part = part * cosine[chunk, :] + other * sine[chunk, :]
                out[chunk, begin : begin + PAIR] = part.astype(out.dtype)


def attend(length, pair, q_begin, rows, q_ref, kn_ref, vn_ref, kc_ref, vc_ref, out_ref):
    fresh = kn_ref.shape[0]
    slots = kc_ref.shape[1]
    block = min(slots, 512)
    lane = lax.broadcasted_iota(jnp.int32, (1, PAIR), 1)
    masks = (lane < HD, lane >= HD)
    cols = pl.ds(pl.multiple_of(pair * PAIR, PAIR), PAIR)
    query = q_ref[pl.ds(pl.multiple_of(q_begin, rows), rows), cols]
    queries = [jnp.where(mask, query, 0) for mask in masks]
    row_index = q_begin + lax.broadcasted_iota(jnp.int32, (rows, 1), 0)

    def absorb(state, keys, values, hide):
        out = []
        for mask, mine, (top, accum) in zip(masks, queries, state):
            scores = lax.dot_general(
                mine, keys, (((1,), (1,)), ((), ())), preferred_element_type=jnp.float32)
            scores = hide(scores * (LOG2E * HD**-0.5))
            new_top = jnp.maximum(top, jnp.max(scores, axis=1, keepdims=True))
            probs = jnp.exp2(scores - new_top).astype(jnp.bfloat16)
            extended = jnp.where(mask, values, 1)
            accum = accum * jnp.exp2(top - new_top) + jnp.dot(
                probs, extended, preferred_element_type=jnp.float32)
            out.append((new_top, accum))
        return tuple(out)

    state = tuple(
        (jnp.full((rows, 1), NEG_FILL, jnp.float32), jnp.zeros((rows, PAIR), jnp.float32)) for _ in masks)

    def fresh_step(index, state):
        begin = pl.multiple_of(index * block, block)
        column = begin + lax.broadcasted_iota(jnp.int32, (1, block), 1)
        return absorb(
            state, kn_ref[pl.ds(begin, block), cols], vn_ref[pl.ds(begin, block), cols],
            lambda scores: jnp.where(row_index >= column, scores, NEG_FILL))

    def cache_step(index, state):
        begin = pl.multiple_of(index * block, block)
        column = begin + lax.broadcasted_iota(jnp.int32, (1, block), 1)
        bias = jnp.where(column < length, 0.0, NEG_FILL)
        return absorb(
            state, kc_ref[0, pl.ds(begin, block)], vc_ref[0, pl.ds(begin, block)],
            lambda scores: scores + bias)

    state = lax.fori_loop(0, fresh // block, fresh_step, state)
    state = lax.fori_loop(0, slots // block, cache_step, state)
    parts = [accum / pltpu.roll(accum, HD, 1) for _, accum in state]
    out_ref[...] = jnp.where(masks[0], parts[0], parts[1]).astype(out_ref.dtype)


QUARTERS = 4
PIECES = 1 + 2 * QUARTERS


def attention_kernel(
    n, n_pairs, n_blocks, length_ref, hidden, gain, w_qkv, cosine, sine, kc_ref, vc_ref, w_out, w_gate, w_up,
    out_ref, keys, values, w_out_full, w_gate_full, w_up_full, queries, *sems
):
    step = pl.program_id(0) * n_blocks + pl.program_id(1)
    steps = n_pairs * n_blocks
    pieces = [(w_out, lambda r: columns_of(w_out_full, r, w_out.shape[1]))]
    for src, full in ((w_gate, w_gate_full), (w_up, w_up_full)):
        depth = src.shape[0]
        for part in range(QUARTERS):
            rows = depth // QUARTERS
            pieces.append((
                src.at[pl.ds(part * rows, rows)],
                lambda r, full=full, part=part, depth=depth, rows=rows: full.at[
                    pl.ds(pl.multiple_of(r * depth + part * rows, rows), rows)]))
    gather = Chain(n, pieces, sems)

    @pl.when(step == 0)
    def _():
        barrier = pltpu.get_barrier_semaphore()
        pl.semaphore_wait(barrier, gather.greet(barrier))
        gather.start()
        project(hidden, gain, w_qkv, cosine, sine, queries, keys, values)

    rows = out_ref.shape[0]
    attend(
        length_ref[0], pl.program_id(0), pl.program_id(1) * rows, rows, queries, keys, values, kc_ref, vc_ref,
        out_ref)

    for t in range(gather.ticks):
        @pl.when(step == min(t, steps - 1))
        def _(t=t):
            gather.tick(t)

    @pl.when(step == steps - 1)
    def _():
        gather.finish()


def attend_and_gather(n, length, hidden, gain, w_qkv, cosine, sine, k_cache, v_cache, w_out, w_gate, w_up):
    rows, features = hidden.shape
    width = w_qkv.shape[2]
    slots = k_cache.shape[1]
    n_pairs, n_blocks = width // PAIR, 2
    hbm = pl.BlockSpec(memory_space=pl.ANY)
    row_block = pl.BlockSpec((rows // n_blocks, PAIR), lambda h, i: (i, h))
    cached = pl.BlockSpec((1, slots, PAIR), lambda h, i: (0, 0, h))

    def whole(*shape):
        return pl.BlockSpec(shape, lambda h, i: (0,) * len(shape), pipeline_mode=pl.Buffered(1))

    fresh = pl.BlockSpec((rows, width), lambda h, i: (0, 0))
    like, bf16 = jax.ShapeDtypeStruct, jnp.bfloat16
    return pl.pallas_call(
        functools.partial(attention_kernel, n, n_pairs, n_blocks),
        grid=(n_pairs, n_blocks),
        out_shape=(
            like((rows, width), bf16),
            like((rows, width), bf16),
            like((rows, width), bf16),
            like((w_out.shape[0], w_out.shape[1] * n), w_out.dtype),
            like((w_gate.shape[0] * n, w_gate.shape[1]), w_gate.dtype),
            like((w_up.shape[0] * n, w_up.shape[1]), w_up.dtype),
        ),
        in_specs=[
            pl.BlockSpec(memory_space=pltpu.SMEM), whole(rows, features), whole(1, features),
            whole(*w_qkv.shape), whole(rows, PAIR), whole(rows, PAIR), cached, cached,
        ] + [hbm] * 3,
        out_specs=(row_block, fresh, fresh) + (hbm,) * 3,
        scratch_shapes=[pltpu.VMEM((rows, width), bf16)] + gather_sems(PIECES, n),
        compiler_params=pltpu.CompilerParams(
            collective_id=1, has_side_effects=True, vmem_limit_bytes=56 * 1024 * 1024,
            dimension_semantics=("arbitrary", "arbitrary")),
    )(length, hidden, gain.reshape(1, features), w_qkv, cosine, sine, k_cache, v_cache, w_out, w_gate, w_up)


CHUNKS = 4
DOWN_PIECES = 8


class Reduce:
    def __init__(self, n, part, near_in, far_out, far_in, sems):
        self.half, self.part, self.near_in, self.far_out, self.far_in = n // 2, part, near_in, far_out, far_in
        self.near_send, self.near_recv, self.far_send, self.far_recv = sems
        self.me = lax.axis_index("mp")
        self.group, self.parity = self.me // 2, lax.rem(self.me, 2)
        self.partner = self.me + 1 - 2 * self.parity
        self.width = part.shape[1] // n
        self.rows = part.shape[0] // CHUNKS

    def rows_of(self, c):
        return pl.ds(c * self.rows, self.rows)

    def block(self, c, index):
        return self.part.at[
            self.rows_of(c), pl.ds(pl.multiple_of(index * self.width, self.width), self.width)]

    def near(self, c, g):
        return pltpu.make_async_remote_copy(
            src_ref=self.block(c, g * 2 + 1 - self.parity), dst_ref=self.near_in.at[g, self.rows_of(c)],
            send_sem=self.near_send.at[c, g], recv_sem=self.near_recv.at[c, g],
            device_id={"mp": self.partner}, device_id_type=MESH)

    def far(self, c, shift):
        target = lax.rem(self.group + shift, self.half)
        return pltpu.make_async_remote_copy(
            src_ref=self.far_out.at[shift, self.rows_of(c)], dst_ref=self.far_in.at[shift, self.rows_of(c)],
            send_sem=self.far_send.at[c, shift], recv_sem=self.far_recv.at[c, shift],
            device_id={"mp": target * 2 + self.parity}, device_id_type=MESH)

    def start(self, c):
        for g in range(self.half):
            self.near(c, g).start()

    def pair_sum(self, c, group):
        return self.block(c, group * 2 + self.parity)[...].astype(jnp.float32) + self.near_in[
            group, self.rows_of(c)].astype(jnp.float32)

    def send_sums(self, c):
        for g in range(self.half):
            self.near(c, g).wait_recv()
        for shift in range(1, self.half):
            target = lax.rem(self.group + shift, self.half)
            self.far_out[shift, self.rows_of(c)] = self.pair_sum(c, target).astype(jnp.bfloat16)
            self.far(c, shift).start()

    def total(self, c):
        value = self.pair_sum(c, self.group)
        for shift in range(1, self.half):
            self.far(c, shift).wait_recv()
            value = value + self.far_in[shift, self.rows_of(c)].astype(jnp.float32)
        return value

    def finish(self, c):
        for g in range(self.half):
            self.near(c, g).wait_send()
        for shift in range(1, self.half):
            self.far(c, shift).wait_send()


def reduce_scratch(rows, width, n):
    dma = pltpu.SemaphoreType.DMA((CHUNKS, n // 2))
    buffers = [pltpu.VMEM((rows, width * n), jnp.bfloat16)] + [
        pltpu.VMEM((n // 2, rows, width), jnp.bfloat16) for _ in range(3)]
    return buffers + [dma] * 4


def dot_tiles(left, right, out, rows):
    columns = out.shape[1]
    tile = min(columns, 512)

    @pl.loop(0, columns // tile)
    def _(index):
        cols = pl.ds(pl.multiple_of(index * tile, tile), tile)
        out[rows, cols] = jnp.dot(
            left[rows, :], right[:, cols], preferred_element_type=jnp.float32).astype(out.dtype)


def middle_kernel(
    n, n_mp, attn, w_out, hidden, gain, w_gate_full, w_up_full, w_down, mid_out, units, w_down_full,
    gate_in, up_in, load_sems, normed, mid_full, part, near_in, far_out, far_in, *sems
):
    rows, width = hidden.shape
    step = rows // CHUNKS
    piece_rows, piece_width = w_down.shape[0] // DOWN_PIECES, w_down.shape[1]
    pieces = [
        (w_down.at[pl.ds(p * piece_rows, piece_rows)],
         lambda r, p=p: w_down_full.at[
             pl.ds(p * piece_rows, piece_rows), pl.ds(pl.multiple_of(r * piece_width, piece_width), piece_width)])
        for p in range(DOWN_PIECES)
    ]
    reduce = Reduce(n_mp, part, near_in, far_out, far_in, sems[:4])
    me = reduce.me

    def mid_block(c, r):
        return mid_full.at[pl.ds(c * step, step), pl.ds(pl.multiple_of(r * width, width), width)]

    down = Chain(n, pieces, sems[4:9])
    spread = Gather(
        "mp", n_mp, [(mid_block(c, me), lambda r, c=c: mid_block(c, r)) for c in range(CHUNKS)],
        sems[9:13] + (None,))
    barrier = pltpu.get_barrier_semaphore()
    pl.semaphore_wait(barrier, down.greet(barrier) + spread.greet(barrier))
    down.start()
    loads = [
        pltpu.make_async_copy(w_gate_full, gate_in, load_sems.at[0]),
        pltpu.make_async_copy(w_up_full, up_in, load_sems.at[1]),
    ]
    for load in loads:
        load.start()

    def chunk_rows(c):
        return pl.ds(c * step, step)

    def mid_chunk(c):
        value = (hidden[chunk_rows(c)].astype(jnp.float32) + reduce.total(c)).astype(jnp.bfloat16)
        mid_block(c, me)[...] = value
        mid_out[chunk_rows(c)] = value
        spread.start(c)

    for c in range(CHUNKS + 3):
        if c < CHUNKS:
            dot_tiles(attn, w_out, part, chunk_rows(c))
            reduce.start(c)
        if 1 <= c <= CHUNKS:
            reduce.send_sums(c - 1)
        if 2 <= c <= CHUNKS + 1:
            mid_chunk(c - 2)
        if 3 <= c:
            spread.forward(c - 3)
        if 1 <= c:
            down.tick(c - 1)
    for load in loads:
        load.wait()
    columns = units.shape[1]
    tile = min(columns, 512)
    for c in range(CHUNKS):
        for shift in range(spread.half):
            spread.near(c, shift).wait_recv()
        values = mid_full[chunk_rows(c)].astype(jnp.float32)
        meansq = jnp.mean(values * values, axis=-1, keepdims=True)
        normed[...] = (values * lax.rsqrt(meansq + EPSILON) * gain[...].astype(jnp.float32)).astype(jnp.bfloat16)

        @pl.loop(0, columns // tile)
        def _(index, c=c):
            cols = pl.ds(pl.multiple_of(index * tile, tile), tile)
            gate = jnp.dot(normed[...], gate_in[:, cols], preferred_element_type=jnp.float32)
            upper = jnp.dot(normed[...], up_in[:, cols], preferred_element_type=jnp.float32)
            units[chunk_rows(c), cols] = (gate * jax.nn.sigmoid(gate) * upper).astype(units.dtype)

        down.tick(CHUNKS + 2 + c)
    for t in range(2 * CHUNKS + 2, down.ticks):
        down.tick(t)
    for c in range(CHUNKS):
        reduce.finish(c)
        for shift in range(1, spread.half):
            spread.far(c, shift).wait_send()
        for shift in range(spread.half):
            spread.near(c, shift).wait_send()
    down.finish()


def middle(n, n_mp, attn, w_out_full, hidden_in, gain, w_gate_full, w_up_full, w_down):
    rows, width = hidden_in.shape
    features = width * n_mp
    vmem, hbm = pl.BlockSpec(memory_space=pltpu.VMEM), pl.BlockSpec(memory_space=pl.ANY)
    like, bf16 = jax.ShapeDtypeStruct, jnp.bfloat16
    dma = pltpu.SemaphoreType.DMA
    return pl.pallas_call(
        functools.partial(middle_kernel, n, n_mp),
        out_shape=(
            like((rows, width), bf16),
            like((rows, w_gate_full.shape[1]), bf16),
            like((w_down.shape[0], w_down.shape[1] * n), bf16),
        ),
        in_specs=[vmem] * 4 + [hbm] * 3,
        out_specs=(vmem, vmem, hbm),
        scratch_shapes=[pltpu.VMEM(w_gate_full.shape, bf16), pltpu.VMEM(w_up_full.shape, bf16), dma((2,))]
        + [pltpu.VMEM((rows // CHUNKS, features), bf16), pltpu.VMEM((rows, features), bf16)]
        + reduce_scratch(rows, width, n_mp) + gather_sems(DOWN_PIECES, n)
        + [dma((CHUNKS, n_mp // 2)) for _ in range(4)],
        compiler_params=pltpu.CompilerParams(
            collective_id=2, has_side_effects=True, vmem_limit_bytes=56 * 1024 * 1024),
    )(attn, w_out_full, hidden_in, gain.reshape(1, features), w_gate_full, w_up_full, w_down)


def last_kernel(n_mp, units, w_down, mid, out, part, near_in, far_out, far_in, *sems):
    rows = mid.shape[0]
    step = rows // CHUNKS
    reduce = Reduce(n_mp, part, near_in, far_out, far_in, sems)
    barrier = pltpu.get_barrier_semaphore()
    for shift in range(1, reduce.half):
        target = lax.rem(reduce.group + shift, reduce.half) * 2 + reduce.parity
        pl.semaphore_signal(barrier, inc=1, device_id={"mp": target}, device_id_type=MESH)
    pl.semaphore_signal(barrier, inc=1, device_id={"mp": reduce.partner}, device_id_type=MESH)
    pl.semaphore_wait(barrier, reduce.half)
    for c in range(CHUNKS + 2):
        if c < CHUNKS:
            dot_tiles(units, w_down, part, pl.ds(c * step, step))
            reduce.start(c)
        if 1 <= c <= CHUNKS:
            reduce.send_sums(c - 1)
        if 2 <= c:
            chunk = pl.ds((c - 2) * step, step)
            out[chunk] = (mid[chunk].astype(jnp.float32) + reduce.total(c - 2)).astype(out.dtype)
    for c in range(CHUNKS):
        reduce.finish(c)


def last(n_mp, units, w_down_full, mid):
    rows, width = mid.shape
    vmem = pl.BlockSpec(memory_space=pltpu.VMEM)
    return pl.pallas_call(
        functools.partial(last_kernel, n_mp),
        out_shape=jax.ShapeDtypeStruct((rows, width), jnp.bfloat16),
        in_specs=[vmem] * 3,
        out_specs=vmem,
        scratch_shapes=reduce_scratch(rows, width, n_mp),
        compiler_params=pltpu.CompilerParams(
            collective_id=3, has_side_effects=True, vmem_limit_bytes=48 * 1024 * 1024),
    )(units, w_down_full, mid)


def on_device(
    n, n_mp, hidden_in, w_qkv, w_out, attn_gain, mlp_gain, w_gate, w_up, w_down, k_cache, v_cache, cache_len
):
    new_count = hidden_in.shape[0]
    full_rows, w_qkv_full = gather_first(n, n_mp, hidden_in, w_qkv)
    positions = (cache_len[0] + jnp.arange(new_count, dtype=jnp.int32)).astype(jnp.float32)
    cosine, sine = rotation(positions)
    attn, fresh_keys, fresh_values, w_out_full, w_gate_full, w_up_full = attend_and_gather(
        n, cache_len, full_rows, attn_gain, w_qkv_full, cosine, sine, k_cache, v_cache, w_out, w_gate, w_up)
    mid_local, units, w_down_full = middle(
        n, n_mp, attn, w_out_full, hidden_in, mlp_gain, w_gate_full, w_up_full, w_down)
    hidden_out = last(n_mp, units, w_down_full, mid_local)
    return hidden_out, fresh_keys, fresh_values


def solution(mesh):
    return jax.shard_map(
        functools.partial(on_device, mesh.shape["req"], mesh.shape["mp"]),
        mesh=mesh,
        in_specs=(
            P("req", "mp"),
            P(None, "req", "mp"),
            P("mp", "req"),
            P(),
            P(),
            P("req", "mp"),
            P("req", "mp"),
            P("mp", "req"),
            P("req", None, "mp"),
            P("req", None, "mp"),
            P("req"),
        ),
        out_specs=(P("req", "mp"), P("req", "mp"), P("req", "mp")),
        check_vma=False,
    )
```
